256 devices in a mesh: subj: 8 (over y, core), slab: 32 (over z, x).
Axes of the slice: x: 4, y: 4, z: 8, core: 2. Of those that a mesh axis runs over, the one named last changes fastest.
Arguments:
- template: float32 [64, 256, 512], P('slab'), may hold values from -6 to 6
- images: float32 [8, 64, 256, 512], P('subj', 'slab'), may hold values from -6 to 6
- fractions: bfloat16 [8, 3, 64, 256, 512], P('subj', None, 'slab'), may hold values from 0 to 1
- requests: int32 [8, 32, 9, 128], P('subj', 'slab'), may hold values from 0 to 511, as said below
- corners: int32 [8, 4, 64, 256], P('subj', None, 'slab'), may hold values from 0 to 1151, as said below
Outputs:
- new_template: float32 [64, 256, 512], P('slab')
- image_force: float32 [8, 3, 64, 256, 512], P('subj', None, 'slab')
The draws below stay inside these ranges and needn't reach their ends.
Inputs may be any that keep to these rules, and one draw needn't show every extreme that they name: requests[s, d, j, c] is a line of source slab device d + j - 4, numbered plane * 256 + row within its 2 planes; the 128 lines of one list are distinct; lists whose source lies outside the grid are never used. corners[s, k, z, x] is a slot j * 128 + c with d + j - 4 a slab device of the grid, d = z // 2; for each subject every such slot of a destination device is named by at least one corner.
All inputs are finite; a program needn't handle non-finite values.
Results may differ from the reference program's by a relative error of at most 0.0003.
Values sent between devices are 32-bit elements; how exact they have to be, the bound alone decides.
No kernel may reach another device: no remote copies, remote signals or barrier semaphores. Data moves between devices by JAX's collectives and lax.ppermute only.
A program may use at most 64 MiB of HBM per device.

```python
import jax
import jax.numpy as jnp
from jax import lax

NX = 256
NY = 512
PLANES = 2
SMOOTH = 2
REACH = 4
BAND = 9
CAP = 128
NZ = 64
SUBJECTS = 8
N_SLAB = 32


def tiled_orders(key, groups, length, total):
    copies = -(-total // length)
    subkeys = jax.random.split(key, groups * copies)
    orders = jax.vmap(lambda one_key: jax.random.permutation(one_key, length))(subkeys)
    return orders.reshape(groups, copies * length)[:, :total].astype(jnp.int32)


def draw_requests(key, part):
    key = jax.random.fold_in(key, 11)
    subkeys = jax.random.split(key, SUBJECTS * N_SLAB * BAND)
    orders = jax.vmap(lambda one_key: jax.random.permutation(one_key, PLANES * NX))(subkeys)
    return orders[:, :CAP].astype(jnp.int32).reshape(SUBJECTS, N_SLAB, BAND, CAP)


def draw_corners(key, part):
    key = jax.random.fold_in(key, 12)
    orders = tiled_orders(key, SUBJECTS * N_SLAB, BAND * CAP, 4 * PLANES * NX)
    layout = orders.reshape(SUBJECTS, N_SLAB, 4 * PLANES * NX)
    band_ids = layout // CAP
    place_ids = layout % CAP
    dest_ids = jnp.arange(N_SLAB, dtype=jnp.int32)[None, :, None]
    owner_ids = jnp.clip(dest_ids + band_ids - REACH, 0, N_SLAB - 1)
    slot_ids = (owner_ids - dest_ids + REACH) * CAP + place_ids
    slot_ids = slot_ids.reshape(SUBJECTS, N_SLAB, 4, PLANES, NX)
    return jnp.transpose(slot_ids, (0, 2, 1, 3, 4)).reshape(SUBJECTS, 4, NZ, NX).astype(jnp.int32)


def shard_levels(rng, shape, cuts, smallest, high):
    gain, own = 1.0, jax.random.fold_in(rng, 6)
    for axis_at, shards_of in cuts:
        draws = jnp.exp(jax.random.uniform(jax.random.fold_in(own, axis_at), (shards_of,), jnp.float32, smallest / len(cuts), high / len(cuts)))
        gain = gain * jnp.repeat(draws, shape[axis_at] // shards_of).reshape([-1 if axis == axis_at else 1 for axis in range(len(shape))])
    return gain


def normal_values(own_key, extent, width, limit, shards=(), kind=jnp.bfloat16):
    entries = width * jax.random.normal(own_key, extent, jnp.float32)
    if shards:
        entries = entries * shard_levels(own_key, extent, shards, -0.22, 0.18)
    return jnp.clip(entries, -limit, limit).astype(kind)


def setup_inputs(seed: int = 0) -> dict:
    streams_of = jax.random.split(jax.random.key(seed), 6)
    template = normal_values(streams_of[0], (NZ, NX, NY), 1.0, 6.0, ((0, 32),), jnp.float32)
    images = normal_values(streams_of[1], (SUBJECTS, NZ, NX, NY), 1.0, 6.0, ((0, 8), (1, 32)), jnp.float32)
    fractions = jnp.clip(1.0 * jax.random.uniform(streams_of[2], (SUBJECTS, 3, NZ, NX, NY), jnp.float32) ** shard_levels(streams_of[2], (SUBJECTS, 3, NZ, NX, NY), ((0, 8), (2, 32)), -0.2, 0.2), 0.0, 1.0).astype(jnp.bfloat16)
    requests = draw_requests(jax.random.fold_in(streams_of[5], 71), 0)
    corners = draw_corners(jax.random.fold_in(streams_of[5], 71), 0)
    return {"template": template, "images": images, "fractions": fractions, "requests": requests, "corners": corners}


diffusion = 0.15


def relax_once(field):
    padded = jnp.pad(field, 1)
    beside = padded[2:, 1:-1, 1:-1] + padded[:-2, 1:-1, 1:-1]
    beside = beside + padded[1:-1, 2:, 1:-1] + padded[1:-1, :-2, 1:-1]
    beside = beside + padded[1:-1, 1:-1, 2:] + padded[1:-1, 1:-1, :-2]
    return field + diffusion * (beside - 6.0 * field)


def reference(template, images, fractions, requests, corners):
    line_total = NZ * NX
    slab_lines = PLANES * NX
    flat_template = template.reshape(line_total, NY)
    dest_ids = jnp.arange(N_SLAB, dtype=jnp.int32)[None, :, None]

    def one_subject(grad_sum, inputs):
        image_one, fraction, request, corner = inputs
        slot_ids = corner.reshape(4, N_SLAB, slab_lines)
        band_ids = slot_ids // CAP
        place_ids = slot_ids % CAP
        owner_ids = dest_ids + band_ids - REACH
        global_line = (owner_ids * slab_lines + request[dest_ids, band_ids, place_ids]).reshape(4, line_total)
        corner_lines = jnp.take(flat_template, global_line, axis=0)
        fraction_f = fraction.astype(jnp.float32).reshape(3, line_total, NY)
        depth_part = fraction_f[0]
        row_part = fraction_f[1]
        across = fraction_f[2]
        weights = jnp.stack([(1.0 - depth_part) * (1.0 - row_part), (1.0 - depth_part) * row_part,
                             depth_part * (1.0 - row_part), depth_part * row_part], axis=0)
        shifted = jnp.concatenate([corner_lines[..., 1:], jnp.zeros_like(corner_lines[..., :1])], axis=-1)
        warped = jnp.sum(weights * ((1.0 - across) * corner_lines + across * shifted), axis=0)
        mismatch = warped - image_one.reshape(line_total, NY)
        volume = warped.reshape(NZ, NX, NY)
        depth_pad = jnp.pad(volume, ((1, 1), (0, 0), (0, 0)))
        row_pad = jnp.pad(volume, ((0, 0), (1, 1), (0, 0)))
        cell_pad = jnp.pad(volume, ((0, 0), (0, 0), (1, 1)))
        depth_diff = 0.5 * (depth_pad[2:] - depth_pad[:-2])
        row_diff = 0.5 * (row_pad[:, 2:] - row_pad[:, :-2])
        cell_diff = 0.5 * (cell_pad[..., 2:] - cell_pad[..., :-2])
        negative = -mismatch.reshape(NZ, NX, NY)
        image_force = jnp.stack([negative * depth_diff, negative * row_diff, negative * cell_diff], axis=0)
        scaled = weights * mismatch[None]
        pushed = (1.0 - across) * scaled + jnp.concatenate(
            [jnp.zeros_like(scaled[..., :1]), (across * scaled)[..., :-1]], axis=-1)
        grad_sum = grad_sum + jax.ops.segment_sum(pushed.reshape(4 * line_total, NY), global_line.reshape(-1),
                                                  num_segments=line_total)
        return grad_sum, image_force

    grad_sum, image_force = lax.scan(one_subject, jnp.zeros((line_total, NY), jnp.float32),
                                     (images, fractions, requests, corners))
    smoothed = grad_sum.reshape(NZ, NX, NY)
    for repeat in range(SMOOTH):
        smoothed = relax_once(smoothed)
    return template - smoothed / SUBJECTS, image_force
```

```python
import functools

import jax
import jax.numpy as jnp
from jax import lax
from jax.experimental import pallas as pl
from jax.experimental.pallas import tpu as pltpu
from jax.sharding import PartitionSpec as P

SMOOTH = 2
REACH = 4
RING = 4
diffusion = 0.15
HALO = SMOOTH

F32 = jnp.float32
BF16 = jnp.bfloat16
I32 = jnp.int32
VMEM = pl.BlockSpec(memory_space=pltpu.VMEM)
SMEM = pl.BlockSpec(memory_space=pltpu.SMEM)
ANY = pl.BlockSpec(memory_space=pl.ANY)
LIMIT = 48 * 2**20


def call(body, outs, in_specs, out_specs, scratch=(), cost=2**20):
    return pl.pallas_call(
        body,
        out_shape=outs,
        in_specs=in_specs,
        out_specs=out_specs,
        scratch_shapes=list(scratch),
        compiler_params=pltpu.CompilerParams(vmem_limit_bytes=LIMIT),
        cost_estimate=pl.CostEstimate(flops=cost, bytes_accessed=cost, transcendentals=0),
    )


def f32s(*shape):
    return jax.ShapeDtypeStruct(shape, F32)


def along_x(value, step):
    count = lax.axis_size("slab")
    route = [(i, i // RING * RING + (i + step) % RING) for i in range(count)]
    return lax.ppermute(value, "slab", route)


def along_slab(value, step):
    count = lax.axis_size("slab")
    return lax.ppermute(value, "slab", [(i, (i + step) % count) for i in range(count)])


def along_z(value, step):
    return along_slab(value, RING * step)


def other_core(value):
    count = lax.axis_size("subj")
    return lax.ppermute(value, "subj", [(i, i ^ 1) for i in range(count)])


def along_y(value, step):
    count = lax.axis_size("subj")
    return lax.ppermute(value, "subj", [(i, (i + 2 * step) % count) for i in range(count)])


def copy_lines(list_ref, list_row, source_ref, out_ref, flip, base):
    capacity = out_ref.shape[0]

    def group(block, carry):
        for unit in range(8):
            place = block * 8 + unit
            line = (list_ref[list_row, place] ^ flip) + base
            out_ref[pl.ds(place, 1), :] = source_ref[pl.ds(line, 1), :]
        return carry

    lax.fori_loop(0, capacity // 8, group, 0)


def own_lines_kernel(place_ref, lists_0, lists_1, lists_2, lists_3, lines_ref, out_0, out_1, out_2, out_3):
    here = place_ref[0]
    for step, lists, out in ((0, lists_0, out_0), (1, lists_1, out_1), (2, lists_2, out_2), (3, lists_3, out_3)):
        there = lax.rem(here + step, RING)
        copy_lines(lists, here - there + REACH, lines_ref, out, 0, 0)


def cross_lines_kernel(
    place_ref, lists_0, lists_1, lists_2, lists_3, low_a, low_b, high_a, high_b,
    out_low, out_high, out_1, out_2, out_3, held, sems,
):
    here = place_ref[0]
    half = low_a.shape[0]
    flip = place_ref[1] * half
    copies = [
        pltpu.make_async_copy(part, held.at[pl.ds(at * half, half)], sems.at[at])
        for at, part in enumerate((low_a, low_b, high_a, high_b))
    ]
    for copy in copies:
        copy.start()
    for copy in copies:
        copy.wait()
    copy_lines(lists_0, 0, held, out_low, flip, 0)
    copy_lines(lists_0, 2 * REACH, held, out_high, flip, 2 * half)
    for step, lists, out in ((1, lists_1, out_1), (2, lists_2, out_2), (3, lists_3, out_3)):
        there = lax.rem(here + step, RING)
        above = (there > here).astype(I32)
        copy_lines(lists, here - there + 2 * REACH * above, held, out, flip, 2 * half * above)


def split_parts(value):
    high = value.astype(BF16)
    low = (value - high.astype(F32)).astype(BF16)
    return high, low


def shift_down(value):
    width = value.shape[1]
    lane = lax.broadcasted_iota(I32, value.shape, 1)
    return jnp.where(lane == width - 1, 0.0, pltpu.roll(value, width - 1, 1))


def shift_up(value):
    lane = lax.broadcasted_iota(I32, value.shape, 1)
    return jnp.where(lane == 0, 0.0, pltpu.roll(value, 1, 1))


def warp_kernel(*refs):
    slot_ref, ids_ref, fraction_ref, image_ref = refs[:4]
    blocks = refs[4:13]
    warped_refs = refs[13:15]
    pooled_refs = refs[15:24]
    held, stage, push_high, push_low, sems = refs[24:]
    capacity = blocks[0].shape[0]
    line_count = image_ref.shape[0]
    rows_plane = line_count // 2
    rows = 16
    copies = [
        pltpu.make_async_copy(block, held.at[pl.ds(at * capacity, capacity)], sems.at[at])
        for at, block in enumerate(blocks)
    ]
    for copy in copies:
        copy.start()
    for copy in copies:
        copy.wait()

    for plane in range(2):
        def step(block, carry):
            local = pl.multiple_of(block * rows, rows)
            first = pl.multiple_of(plane * rows_plane + block * rows, rows)
            for corner in range(4):
                for row in range(rows):
                    line = slot_ref[corner, first + row]
                    stage[pl.ds(corner * rows + row, 1), :] = held[pl.ds(line, 1), :]
            depth_part = fraction_ref[0, pl.ds(first, rows), :].astype(F32)
            row_part = fraction_ref[1, pl.ds(first, rows), :].astype(F32)
            across = fraction_ref[2, pl.ds(first, rows), :].astype(F32)
            depth_rest, row_rest, rest = 1.0 - depth_part, 1.0 - row_part, 1.0 - across
            weights = (
                depth_rest * row_rest, depth_rest * row_part,
                depth_part * row_rest, depth_part * row_part,
            )
            warped = None
            for corner in range(4):
                lines = stage[corner * rows:(corner + 1) * rows, :]
                term = weights[corner] * (rest * lines + across * shift_down(lines))
                warped = term if warped is None else warped + term
            warped_refs[plane][pl.ds(local, rows), :] = warped
            mismatch = warped - image_ref[pl.ds(first, rows), :]
            for corner in range(4):
                scaled = weights[corner] * mismatch
                pushed = rest * scaled + shift_up(across * scaled)
                high, low = split_parts(pushed)
                at = pl.multiple_of(corner * line_count + plane * rows_plane + block * rows, rows)
                push_high[pl.ds(at, rows), :] = high
                push_low[pl.ds(at, rows), :] = low
            return carry

        lax.fori_loop(0, rows_plane // rows, step, 0)

    group = 3
    total = 4 * line_count
    slot = lax.broadcasted_iota(I32, (group * capacity, total), 0)
    for first in range(0, 9, group):
        chosen = (ids_ref[...] == slot + first * capacity)
        hot = jnp.where(chosen, 1.0, 0.0).astype(BF16)
        summed = jnp.dot(hot, push_high[...], preferred_element_type=F32)
        summed = summed + jnp.dot(hot, push_low[...], preferred_element_type=F32)
        for at in range(group):
            pooled_refs[first + at][...] = summed[at * capacity:(at + 1) * capacity]


def add_lines(target_rows, ids, values, outs):
    high_refs, low_refs = values
    for out, first, count in outs:
        hot = jnp.where(target_rows[first:first + count] == ids, 1.0, 0.0).astype(BF16)
        out[...] = jnp.dot(hot, high_refs, preferred_element_type=F32) + jnp.dot(
            hot, low_refs, preferred_element_type=F32
        )


def own_back_kernel(
    place_ref, lists_0, lists_1, lists_2, lists_3, rows_ref, in_0, in_1, in_2, in_3, keep, send
):
    here = place_ref[0]
    ids = []
    for step, lists in enumerate((lists_0, lists_1, lists_2, lists_3)):
        there = lax.rem(here + step, RING)
        ids.append(lists[pl.ds(here - there + REACH, 1), :])
    values = jnp.concatenate([in_0[...], in_1[...], in_2[...], in_3[...]], axis=0)
    count = keep.shape[0]
    add_lines(rows_ref[...], jnp.concatenate(ids, axis=1), split_parts(values),
              ((keep, 0, count), (send, count, count)))


def cross_back_kernel(
    place_ref, lists_0, lists_1, lists_2, lists_3, rows_ref, in_low, in_high, in_1, in_2, in_3,
    keep_low, keep_high, send_low, send_high,
):
    here = place_ref[0]
    span = 2 * REACH * in_low.shape[0]
    ids = [lists_0[0:1, :], lists_0[2 * REACH:2 * REACH + 1, :] + span]
    for step, lists in enumerate((lists_1, lists_2, lists_3), 1):
        there = lax.rem(here + step, RING)
        above = (there > here).astype(I32)
        ids.append(lists[pl.ds(here - there + 2 * REACH * above, 1), :] + span * above)
    ids = jnp.concatenate(ids, axis=1)
    values = split_parts(jnp.concatenate([in_low[...], in_high[...], in_1[...], in_2[...], in_3[...]], axis=0))
    count = keep_low.shape[0]
    rows = rows_ref[...]
    add_lines(rows, ids, values, ((keep_low, 0, count), (send_low, count, count)))
    add_lines(rows, ids - span, values, ((keep_high, 0, count), (send_high, count, count)))


def smooth_kernel(place_ref, before, piece, after, template_ref, out, field):
    device, last, core, chip = place_ref[2], place_ref[3], place_ref[1], place_ref[4]
    size = piece.shape[0]
    rows = size // 2
    total = 3 * size
    zero = jnp.zeros(piece.shape, F32)
    field[0:size, :] = jnp.where(device > 0, before[...], zero)
    field[size:2 * size, :] = piece[...]
    field[2 * size:3 * size, :] = jnp.where(device < last, after[...], zero)
    width = piece.shape[1]
    at = lax.broadcasted_iota(I32, (total, width), 0)
    row = lax.rem(at, rows)
    per_piece = rows - 2 * HALO
    index = core * RING + chip
    row = row + index * per_piece - HALO
    inside = (row >= 0) & (row < 2 * RING * per_piece)
    inside = inside & ((at >= size) | (device > 0)) & ((at < 2 * size) | (device < last))
    current = field[...]
    for repeat in range(SMOOTH):
        beside = pltpu.roll(current, rows, 0) + pltpu.roll(current, total - rows, 0)
        beside = beside + pltpu.roll(current, 1, 0) + pltpu.roll(current, total - 1, 0)
        beside = beside + shift_up(current) + shift_down(current)
        current = current + diffusion * (beside - 6.0 * current)
        if repeat < SMOOTH - 1:
            current = jnp.where(inside, current, 0.0)
    field[...] = current
    subjects = place_ref[5].astype(F32)
    plane_rows = template_ref.shape[0] // 2
    for plane in range(2):
        start = pl.multiple_of(plane * plane_rows + index * per_piece, per_piece)
        found = field[pl.ds(size + plane * rows + HALO, per_piece), :]
        out[plane * per_piece:(plane + 1) * per_piece, :] = (
            template_ref[pl.ds(start, per_piece), :] - found / subjects
        )


def assemble_kernel(place_ref, *refs):
    pieces, out, sems = refs[:2 * RING], refs[2 * RING], refs[2 * RING + 1]
    core, chip = place_ref[1], place_ref[4]
    count = pieces[0].shape[0] // 2
    plane_rows = out.shape[0] // 2
    copies = []
    for at, piece in enumerate(pieces):
        part = core if at < RING else 1 - core
        index = part * RING + lax.rem(chip + RING - at % RING, RING)
        for plane in range(2):
            start = pl.multiple_of(plane * plane_rows + index * count, count)
            copies.append(
                pltpu.make_async_copy(
                    piece.at[pl.ds(plane * count, count)], out.at[pl.ds(start, count)], sems.at[2 * at + plane]
                )
            )
    for copy in copies:
        copy.start()
    for copy in copies:
        copy.wait()


def force_kernel(place_ref, before, plane_0, plane_1, after, image_ref, out):
    device, last = place_ref[2], place_ref[3]
    rows_plane, width = plane_0.shape
    rows = 32
    row = lax.broadcasted_iota(I32, (rows, width), 0)
    for plane, (previous, current, following) in enumerate(
        ((before, plane_0, plane_1), (plane_0, plane_1, after))
    ):
        def step(block, carry):
            first = pl.multiple_of(block * rows, rows)
            centre = current[pl.ds(first, rows), :]
            negative = image_ref[pl.ds(plane * rows_plane + first, rows), :] - centre
            back, ahead = previous[pl.ds(first, rows), :], following[pl.ds(first, rows), :]
            if plane == 0:
                back = jnp.where(device > 0, back, 0.0)
            else:
                ahead = jnp.where(device < last, ahead, 0.0)
            out[0, plane, pl.ds(first, rows), :] = negative * (0.5 * (ahead - back))
            above = current[pl.ds(jnp.maximum(first - 1, 0), 1), :]
            above = jnp.where(first > 0, above, 0.0)
            below = current[pl.ds(jnp.minimum(first + rows, rows_plane - 1), 1), :]
            below = jnp.where(first + rows < rows_plane, below, 0.0)
            up = jnp.where(row == 0, above, pltpu.roll(centre, 1, 0))
            down = jnp.where(row == rows - 1, below, pltpu.roll(centre, rows - 1, 0))
            out[1, plane, pl.ds(first, rows), :] = negative * (0.5 * (down - up))
            out[2, plane, pl.ds(first, rows), :] = negative * (0.5 * (shift_down(centre) - shift_up(centre)))
            return carry

        lax.fori_loop(0, rows_plane // rows, step, 0)


def on_device(template, images, fractions, requests, corners):
    _, plane_count, row_count, cell_count = images.shape
    line_count = plane_count * row_count
    band_count, capacity = requests.shape[2:]
    slab = lax.axis_index("slab")
    subject = lax.axis_index("subj")
    last = lax.axis_size("slab") - 1
    here = slab % RING
    core = subject % 2
    chip = subject // 2
    place = jnp.stack([here, core, slab, jnp.int32(last), chip, jnp.int32(lax.axis_size("subj"))]).astype(I32)
    lists = requests.reshape(band_count, capacity)
    lines = template.reshape(line_count, cell_count)
    block = f32s(capacity, cell_count)

    asked = [lists] + [along_x(lists, -step) for step in (1, 2, 3)]
    plane = lax.dynamic_index_in_dim(template, core, 0, keepdims=False)
    from_low = along_z(plane, 1)
    from_high = along_z(plane, -1)

    own = call(
        own_lines_kernel, (block,) * 4, [SMEM] * 5 + [VMEM], (VMEM,) * 4
    )(place, *asked, lines)
    got_own = [along_x(own[step], step) for step in (1, 2, 3)]
    from_low_b, from_high_b = other_core(from_low), other_core(from_high)
    cross = call(
        cross_lines_kernel, (block,) * 5, [SMEM] * 5 + [ANY] * 4, (VMEM,) * 5,
        [pltpu.VMEM((2 * line_count, cell_count), F32), pltpu.SemaphoreType.DMA((4,))],
    )(place, *asked, from_low, from_low_b, from_high, from_high_b)
    got_cross = [along_x(cross[1 + step], step) for step in (1, 2, 3)]

    slot_ids = corners.reshape(4, line_count)
    offset = slot_ids // capacity - REACH
    source = here + offset
    outside = (source < 0) | (source >= RING)
    behind = (here - source) % RING
    held_at = jnp.where(
        behind == 0,
        jnp.where(offset == 0, 0, jnp.where(offset < 0, 1, 2)),
        1 + 2 * behind + outside.astype(I32),
    )
    slot_ids = held_at * capacity + slot_ids % capacity

    blocks = [own[0], cross[0], cross[1]]
    for at in range(3):
        blocks += [got_own[at], got_cross[at]]
    half = f32s(row_count, cell_count)
    results = call(
        warp_kernel,
        (half,) * 2 + (block,) * 9,
        [SMEM] + [VMEM] * 3 + [ANY] * 9,
        (VMEM,) * 11,
        [
            pltpu.VMEM((band_count * capacity, cell_count), F32),
            pltpu.VMEM((64, cell_count), F32),
            pltpu.VMEM((4 * line_count, cell_count), BF16),
            pltpu.VMEM((4 * line_count, cell_count), BF16),
            pltpu.SemaphoreType.DMA((9,)),
        ],
        2**24,
    )(
        slot_ids, slot_ids.reshape(1, 4 * line_count),
        fractions.reshape(3, line_count, cell_count), images.reshape(line_count, cell_count), *blocks,
    )
    warped_0, warped_1 = results[:2]
    pooled = results[2:]

    back_cross = [along_x(pooled[2 + 2 * step], -step) for step in (1, 2, 3)]
    back_own = [along_x(pooled[1 + 2 * step], -step) for step in (1, 2, 3)]

    per_piece = row_count // (2 * RING)
    wide = per_piece + 2 * HALO
    at = jnp.arange(2 * RING * 2 * wide, dtype=I32)
    piece = at // (2 * wide)
    part = jnp.where(piece < RING, core, 1 - core)
    index = part * RING + (chip + piece) % RING
    row = index * per_piece - HALO + at % wide
    target = jnp.where((row >= 0) & (row < row_count), at // wide % 2 * row_count + row, -(2**20))
    target = target.reshape(-1, 1)
    core_part = f32s(RING * 2 * wide, cell_count)
    keep_low, keep_high, send_low, send_high = call(
        cross_back_kernel, (core_part,) * 4, [SMEM] + [VMEM] * 10, (VMEM,) * 4, (), 2**22
    )(place, *asked, target, pooled[1], pooled[2], *back_cross)
    sum_low = keep_low + other_core(send_low)
    sum_high = keep_high + other_core(send_high)
    in_from_high = along_z(sum_low, -1)
    in_from_low = along_z(sum_high, 1)
    keep_own, send_own = call(
        own_back_kernel, (core_part,) * 2, [SMEM] + [VMEM] * 9, (VMEM,) * 2, (), 2**22
    )(place, *asked, target, pooled[0], *back_own)
    total = keep_own + other_core(send_own) + in_from_high + in_from_low

    size = 2 * wide
    pieces = [total[at * size:(at + 1) * size] for at in range(RING)]
    piece_sum = pieces[0] + along_y(pieces[1], 1) + along_y(pieces[2], 2) + along_y(pieces[3], 3)
    before, after = along_slab(piece_sum, 1), along_slab(piece_sum, -1)
    new_piece = call(
        smooth_kernel, f32s(2 * per_piece, cell_count), [SMEM] + [VMEM] * 4, VMEM,
        [pltpu.VMEM((3 * size, cell_count), F32)],
    )(place, before, piece_sum, after, lines)

    edge_0, edge_1, _ = lax.optimization_barrier((warped_0, warped_1, keep_own))
    edge_before, edge_after = along_slab(edge_1, 1), along_slab(edge_0, -1)
    image_force = call(
        force_kernel, f32s(3, plane_count, row_count, cell_count), [SMEM] + [VMEM] * 5, VMEM, (), 2**22
    )(place, edge_before, warped_0, warped_1, edge_after, images.reshape(line_count, cell_count))

    mine = [new_piece] + [along_y(new_piece, step) for step in (1, 2, 3)]
    theirs = [other_core(value) for value in mine]
    new_template = call(
        assemble_kernel, f32s(line_count, cell_count), [SMEM] + [ANY] * 8, ANY,
        [pltpu.SemaphoreType.DMA((16,))],
    )(place, *mine, *theirs)
    return new_template.reshape(template.shape), image_force[None]


def solution(mesh):
    return jax.shard_map(
        on_device,
        mesh=mesh,
        in_specs=(
            P("slab", None, None),
            P("subj", "slab", None, None),
            P("subj", None, "slab", None, None),
            P("subj", "slab", None, None),
            P("subj", None, "slab", None),
        ),
        out_specs=(P("slab", None, None), P("subj", None, "slab", None, None)),
        check_vma=False,
    )
```

```python
import functools

import jax
import jax.numpy as jnp
from jax import lax
from jax.experimental import pallas as pl
from jax.experimental.pallas import tpu as pltpu
from jax.sharding import PartitionSpec as P

SMOOTH = 2
REACH = 4
RING = 4
diffusion = 0.15
HALO = SMOOTH
LANES = 128
WARP_ROWS = 32

F32 = jnp.float32
BF16 = jnp.bfloat16
I32 = jnp.int32
VMEM = pl.BlockSpec(memory_space=pltpu.VMEM)
SMEM = pl.BlockSpec(memory_space=pltpu.SMEM)
ANY = pl.BlockSpec(memory_space=pl.ANY)
LIMIT = 8 * 2**20


def call(body, outs, in_specs, out_specs, scratch=(), aliases={}):
    return pl.pallas_call(
        body,
        out_shape=outs,
        in_specs=in_specs,
        out_specs=out_specs,
        scratch_shapes=list(scratch),
        input_output_aliases=aliases,
        compiler_params=pltpu.CompilerParams(vmem_limit_bytes=LIMIT),
    )


def f32s(*shape):
    return jax.ShapeDtypeStruct(shape, F32)


def along_x(value, step):
    count = lax.axis_size("slab")
    route = [(i, i // RING * RING + (i + step) % RING) for i in range(count)]
    return lax.ppermute(value, "slab", route)


def along_slab(value, step):
    count = lax.axis_size("slab")
    return lax.ppermute(value, "slab", [(i, (i + step) % count) for i in range(count)])


def along_z(value, step):
    return along_slab(value, RING * step)


def other_core(value):
    count = lax.axis_size("subj")
    return lax.ppermute(value, "subj", [(i, i ^ 1) for i in range(count)])


def along_y(value, step):
    count = lax.axis_size("subj")
    return lax.ppermute(value, "subj", [(i, (i + 2 * step) % count) for i in range(count)])


def spread_kernel(place_ref, source_ref, all_ref, half_ref):
    count, width = source_ref.shape
    parts = width // LANES
    rows = count // 2

    def group(block, carry):
        first = pl.multiple_of(block * 8, 8)
        for part in range(parts):
            all_ref[pl.ds(first * parts + part, 8, stride=parts), :] = source_ref[
                pl.ds(first, 8), part * LANES:(part + 1) * LANES
            ]
        return carry

    lax.fori_loop(0, count // 8, group, 0, unroll=4)
    unit = 64
    start = place_ref[1] * rows * parts

    def copy(block, carry):
        first = pl.multiple_of(block * unit, unit)
        half_ref[pl.ds(first, unit), :] = all_ref[pl.ds(pl.multiple_of(start + first, unit), unit), :]
        return carry

    lax.fori_loop(0, rows * parts // unit, copy, 0, unroll=4)


def request_kernel(place_ref, lists_ref, self_ref, out_1, out_2, out_3):
    here = place_ref[0]
    line_count = place_ref[6]
    parts = place_ref[7]
    flip = place_ref[1] * (line_count // 2) * parts

    def across(row, above):
        return ((lists_ref[pl.ds(row, 1), :] * parts) ^ flip) + above * line_count * parts

    self_ref[0:1, :] = lists_ref[REACH:REACH + 1, :] * parts
    self_ref[1:2, :] = across(0, 0)
    self_ref[2:3, :] = across(2 * REACH, 1)
    for step, out in ((1, out_1), (2, out_2), (3, out_3)):
        server = lax.rem(here + RING - step, RING)
        above = (here > server).astype(I32)
        out[0:1, :] = lists_ref[pl.ds(server - here + REACH, 1), :] * parts
        out[1:2, :] = across(server - here + 2 * REACH * above, above)


def copy_lines(list_ref, list_row, held, out_ref):
    count = list_ref.shape[1]
    parts = out_ref.shape[0] // count
    unit = 16

    def group(block, carry):
        found = [
            held[pl.ds(pl.multiple_of(list_ref[list_row, block * unit + at], parts), parts), :] for at in range(unit)
        ]
        for at in range(unit):
            place = pl.multiple_of((block * unit + at) * parts, parts)
            out_ref[pl.ds(place, parts), :] = found[at]
        return carry

    lax.fori_loop(0, count // unit, group, 0, unroll=2)


def own_lines_kernel(lists_0, lists_1, lists_2, lists_3, held, out_0, out_1, out_2, out_3):
    for lists, out in ((lists_1, out_1), (lists_2, out_2), (lists_3, out_3), (lists_0, out_0)):
        copy_lines(lists, 0, held, out)


def cross_lines_kernel(
    lists_0, lists_1, lists_2, lists_3, low_a, low_b, high_a, high_b,
    out_low, out_high, out_1, out_2, out_3, held, sems,
):
    size = low_a.shape[0]
    copies = [
        pltpu.make_async_copy(part, held.at[pl.ds(at * size, size)], sems.at[at])
        for at, part in enumerate((low_a, low_b, high_a, high_b))
    ]
    for copy in copies:
        copy.start()
    for copy in copies:
        copy.wait()
    for lists, row, out in (
        (lists_1, 1, out_1), (lists_2, 1, out_2), (lists_3, 1, out_3), (lists_0, 1, out_low), (lists_0, 2, out_high),
    ):
        copy_lines(lists, row, held, out)


def split_parts(value):
    high = value.astype(BF16)
    low = (value - high.astype(F32)).astype(BF16)
    return high, low


def shift_down(value):
    width = value.shape[1]
    lane = lax.broadcasted_iota(I32, value.shape, 1)
    return jnp.where(lane == width - 1, 0.0, pltpu.roll(value, width - 1, 1))


def shift_up(value):
    lane = lax.broadcasted_iota(I32, value.shape, 1)
    return jnp.where(lane == 0, 0.0, pltpu.roll(value, 1, 1))


def corner_parts(scale, depth_part, row_part):
    above, below = scale * depth_part, scale * (1.0 - depth_part)
    rest = 1.0 - row_part
    return below * rest, below * row_part, above * rest, above * row_part


def weight_kernel(fraction_ref, here_ref, ahead_ref):
    line_count, width = fraction_ref.shape[1:]
    rows = 16
    lane = lax.broadcasted_iota(I32, (rows, width), 1)

    def step(block, carry):
        first = pl.multiple_of(block * rows, rows)
        depth_part, row_part, across = [fraction_ref[at, pl.ds(first, rows), :].astype(F32) for at in range(3)]
        here = corner_parts(1.0 - across, depth_part, row_part)
        ahead = corner_parts(
            jnp.where(lane == 0, 0.0, pltpu.roll(across, 1, 1)),
            pltpu.roll(depth_part, 1, 1), pltpu.roll(row_part, 1, 1),
        )
        for corner in range(4):
            here_ref[corner, pl.ds(first, rows), :] = here[corner]
            ahead_ref[corner, pl.ds(first, rows), :] = ahead[corner]
        return carry

    lax.fori_loop(0, line_count // rows, step, 0)


def warp_kernel(*refs):
    slot_ref, here_ref, ahead_ref, image_ref = refs[:4]
    blocks = refs[4:13]
    warped_refs, push_high, push_low = refs[13:15], refs[15], refs[16]
    held, stage_0, stage_1, sems = refs[17:]
    size = blocks[0].shape[0]
    line_count, width = image_ref.shape
    parts = width // LANES
    rows_plane = line_count // 2
    rows = WARP_ROWS
    copies = [
        pltpu.make_async_copy(block, held.at[pl.ds(at * size, size)], sems.at[at])
        for at, block in enumerate(blocks)
    ]
    for copy in copies:
        copy.start()
    for copy in copies:
        copy.wait()

    def gather(block, stage, corner, low, high):
        first = block * rows
        found = []
        for row in range(low, high):
            line = slot_ref[corner, first + row]
            found.append(held[pl.ds(pl.multiple_of(line * parts, parts), parts), :])
        for row in range(low, high):
            at = (corner * rows + row) * parts
            stage[at:at + parts, :] = found[row - low]

    lane = lax.broadcasted_iota(I32, (rows, width), 1)

    def combine(plane, block, stage, following, stage_after):
        first = pl.multiple_of(block * rows, rows)
        near, far = None, None
        for corner in range(4):
            lines = jnp.concatenate(
                [stage[pl.ds(corner * rows * parts + part, rows, stride=parts), :] for part in range(parts)],
                axis=1,
            )
            near_term = here_ref[corner, pl.ds(first, rows), :] * lines
            far_term = ahead_ref[corner, pl.ds(first, rows), :] * lines
            gather(following, stage_after, corner, 0, rows // 2)
            near = near_term if near is None else near + near_term
            far = far_term if far is None else far + far_term
        warped = near + jnp.where(lane == width - 1, 0.0, pltpu.roll(far, width - 1, 1))
        warped_refs[plane][pl.ds(pl.multiple_of(first - plane * rows_plane, rows), rows), :] = warped
        mismatch = warped - image_ref[pl.ds(first, rows), :]
        behind = pltpu.roll(mismatch, 1, 1)
        for corner in range(4):
            here, ahead = here_ref[corner, pl.ds(first, rows), :], ahead_ref[corner, pl.ds(first, rows), :]
            high, low = split_parts(here * mismatch + ahead * behind)
            gather(following, stage_after, corner, rows // 2, rows)
            at = pl.multiple_of(corner * line_count + first, rows)
            push_high[pl.ds(at, rows), :] = high
            push_low[pl.ds(at, rows), :] = low

    blocks_plane = rows_plane // rows
    last = 2 * blocks_plane - 1
    for corner in range(4):
        gather(0, stage_0, corner, 0, rows)
    for plane in range(2):
        def step(pair, carry):
            block = plane * blocks_plane + 2 * pair
            combine(plane, block, stage_0, block + 1, stage_1)
            combine(plane, block + 1, stage_1, jnp.minimum(block + 2, last), stage_0)
            return carry

        lax.fori_loop(0, blocks_plane // 2, step, 0)


def slot_sum_kernel(first, ids_ref, push_high, push_low, *outs):
    capacity = outs[0].shape[0]
    slot = lax.broadcasted_iota(I32, (capacity, push_high.shape[0]), 0)
    for start in range(0, len(outs), 3):
        chosen = outs[start:start + 3]
        hot = jnp.concatenate(
            [
                jnp.where(ids_ref[...] == slot + (first + start + at) * capacity, 1.0, 0.0).astype(BF16)
                for at in range(len(chosen))
            ],
            axis=0,
        )
        summed = jnp.dot(hot, push_high[...], preferred_element_type=F32)
        summed = summed + jnp.dot(hot, push_low[...], preferred_element_type=F32)
        for at, out in enumerate(chosen):
            out[...] = summed[at * capacity:(at + 1) * capacity]


def line_hot_kernel(place_ref, lists_0, lists_1, lists_2, lists_3, rows_ref, own_ref, low_ref, high_ref):
    capacity = lists_0.shape[1]
    line_count, parts = place_ref[6], place_ref[7]
    flip = place_ref[1] * (line_count // 2) * parts
    rows = rows_ref[...] * parts

    def hot(ids):
        return jnp.where(rows == ids, 1.0, 0.0).astype(BF16)

    own_lists = (lists_0[0:1, :], lists_1[0:1, :], lists_2[0:1, :], lists_3[0:1, :])
    cross_lists = (lists_0[1:2, :], lists_0[2:3, :], lists_1[1:2, :], lists_2[1:2, :], lists_3[1:2, :])
    for at, ids in enumerate(own_lists):
        own_ref[:, at * capacity:(at + 1) * capacity] = hot(ids)
    for at, ids in enumerate(cross_lists):
        ids = ids ^ flip
        low_ref[:, at * capacity:(at + 1) * capacity] = hot(ids)
        high_ref[:, at * capacity:(at + 1) * capacity] = hot(ids - line_count * parts)


def line_sums(hot, parts):
    return jnp.dot(hot, parts[0], preferred_element_type=F32) + jnp.dot(hot, parts[1], preferred_element_type=F32)


def own_back_kernel(hot_ref, in_0, in_1, in_2, in_3, keep, send_0, send_1):
    values = split_parts(jnp.concatenate([in_0[...], in_1[...], in_2[...], in_3[...]], axis=0))
    count = keep.shape[0]
    keep[...] = line_sums(hot_ref[:count], values)
    sent = line_sums(hot_ref[count:], values)
    send_0[...] = sent[:count // 2]
    send_1[...] = sent[count // 2:]


def cross_back_kernel(hot_low, hot_high, in_low, in_high, in_1, in_2, in_3, keep_low, keep_high, send):
    values = split_parts(jnp.concatenate([in_low[...], in_high[...], in_1[...], in_2[...], in_3[...]], axis=0))
    count = keep_low.shape[0]
    for at, (hot, keep) in enumerate(((hot_low, keep_low), (hot_high, keep_high))):
        send[at * count:(at + 1) * count] = line_sums(hot[count:], values)
        keep[...] = line_sums(hot[:count], values)


def smooth_kernel(place_ref, before, piece, after, template_ref, out, field):
    device, last, core, chip = place_ref[2], place_ref[3], place_ref[1], place_ref[4]
    size = piece.shape[0]
    rows = size // 2
    total = 3 * size
    zero = jnp.zeros(piece.shape, F32)
    field[0:size, :] = jnp.where(device > 0, before[...], zero)
    field[size:2 * size, :] = piece[...]
    field[2 * size:3 * size, :] = jnp.where(device < last, after[...], zero)
    width = piece.shape[1]
    at = lax.broadcasted_iota(I32, (total, width), 0)
    row = lax.rem(at, rows)
    per_piece = rows - 2 * HALO
    index = core * RING + chip
    row = row + index * per_piece - HALO
    inside = (row >= 0) & (row < 2 * RING * per_piece)
    inside = inside & ((at >= size) | (device > 0)) & ((at < 2 * size) | (device < last))
    current = field[...]
    for repeat in range(SMOOTH):
        beside = pltpu.roll(current, rows, 0) + pltpu.roll(current, total - rows, 0)
        beside = beside + pltpu.roll(current, 1, 0) + pltpu.roll(current, total - 1, 0)
        beside = beside + shift_up(current) + shift_down(current)
        current = current + diffusion * (beside - 6.0 * current)
        if repeat < SMOOTH - 1:
            current = jnp.where(inside, current, 0.0)
    field[...] = current
    subjects = place_ref[5].astype(F32)
    plane_rows = template_ref.shape[0] // 2
    for plane in range(2):
        start = pl.multiple_of(plane * plane_rows + index * per_piece, per_piece)
        found = field[pl.ds(size + plane * rows + HALO, per_piece), :]
        out[plane * per_piece:(plane + 1) * per_piece, :] = (
            template_ref[pl.ds(start, per_piece), :] - found / subjects
        )


def assemble_kernel(place_ref, *refs):
    pieces, out, sems = refs[:2 * RING], refs[2 * RING], refs[2 * RING + 1]
    core, chip = place_ref[1], place_ref[4]
    count = pieces[0].shape[0] // 2
    plane_rows = out.shape[0] // 2
    copies = []
    for at, piece in enumerate(pieces):
        part = core if at < RING else 1 - core
        index = part * RING + lax.rem(chip + RING - at % RING, RING)
        for plane in range(2):
            start = pl.multiple_of(plane * plane_rows + index * count, count)
            copies.append(
                pltpu.make_async_copy(
                    piece.at[pl.ds(plane * count, count)], out.at[pl.ds(start, count)], sems.at[2 * at + plane]
                )
            )
    for copy in copies:
        copy.start()
    for copy in copies:
        copy.wait()


def plane_force_kernel(plane_0, plane_1, image_ref, out, held, sem):
    rows_plane, width = plane_0.shape
    rows = 32
    row = lax.broadcasted_iota(I32, (rows, width), 0)
    for plane, current in enumerate((plane_0, plane_1)):
        def step(block, carry):
            first = pl.multiple_of(block * rows, rows)
            centre = current[pl.ds(first, rows), :]
            negative = image_ref[pl.ds(plane * rows_plane + first, rows), :] - centre
            above = current[pl.ds(jnp.maximum(first - 1, 0), 1), :]
            above = jnp.where(first > 0, above, 0.0)
            below = current[pl.ds(jnp.minimum(first + rows, rows_plane - 1), 1), :]
            below = jnp.where(first + rows < rows_plane, below, 0.0)
            up = jnp.where(row == 0, above, pltpu.roll(centre, 1, 0))
            down = jnp.where(row == rows - 1, below, pltpu.roll(centre, rows - 1, 0))
            held[0, plane, pl.ds(first, rows), :] = negative * (0.5 * (down - up))
            held[1, plane, pl.ds(first, rows), :] = negative * (0.5 * (shift_down(centre) - shift_up(centre)))
            return carry

        lax.fori_loop(0, rows_plane // rows, step, 0)
    copy = pltpu.make_async_copy(held, out.at[pl.ds(1, 2)], sem)
    copy.start()
    copy.wait()


def depth_force_kernel(place_ref, before, plane_0, plane_1, after, image_ref, given, out, held, sem):
    device, last = place_ref[2], place_ref[3]
    rows_plane = plane_0.shape[0]
    rows = 32

    def step(block, carry):
        at = pl.ds(pl.multiple_of(block * rows, rows), rows)
        lower, upper = plane_0[at, :], plane_1[at, :]
        back = jnp.where(device > 0, before[at, :], 0.0)
        ahead = jnp.where(device < last, after[at, :], 0.0)
        image_0 = image_ref[at, :]
        image_1 = image_ref[pl.ds(pl.multiple_of(rows_plane + block * rows, rows), rows), :]
        held[0, 0, at, :] = (image_0 - lower) * (0.5 * (upper - back))
        held[0, 1, at, :] = (image_1 - upper) * (0.5 * (ahead - lower))
        return carry

    lax.fori_loop(0, rows_plane // rows, step, 0)
    copy = pltpu.make_async_copy(held, out.at[pl.ds(0, 1)], sem)
    copy.start()
    copy.wait()


def on_device(template, images, fractions, requests, corners):
    _, plane_count, row_count, cell_count = images.shape
    line_count = plane_count * row_count
    band_count, capacity = requests.shape[2:]
    slab = lax.axis_index("slab")
    subject = lax.axis_index("subj")
    last = lax.axis_size("slab") - 1
    here = slab % RING
    core = subject % 2
    chip = subject // 2
    fixed = [last, lax.axis_size("subj"), line_count, cell_count // LANES]
    place = jnp.stack([here, core, slab, fixed[0], chip, fixed[1], fixed[2], fixed[3]]).astype(I32)
    lists = requests.reshape(band_count, capacity)
    lines = template.reshape(line_count, cell_count)
    parts = cell_count // LANES
    packed = f32s(capacity * parts, LANES)

    spread, plane = call(
        spread_kernel, (f32s(line_count * parts, LANES), f32s(row_count * parts, LANES)), [SMEM, VMEM], (VMEM,) * 2,
    )(place, lines)
    from_low = along_z(plane, 1)
    from_high = along_z(plane, -1)
    message = jax.ShapeDtypeStruct((2, capacity), I32)
    self_lists, *messages = call(
        request_kernel, (jax.ShapeDtypeStruct((3, capacity), I32),) + (message,) * 3, [SMEM, VMEM], (VMEM,) * 4,
    )(place, lists)
    asked = [self_lists] + [along_x(messages[step - 1], -step) for step in (1, 2, 3)]

    own = call(
        own_lines_kernel, (packed,) * 4, [SMEM] * 4 + [VMEM], (VMEM,) * 4,
    )(*asked, spread)
    got_own = [along_x(own[step], step) for step in (1, 2, 3)]
    from_low, from_high, _ = lax.optimization_barrier((from_low, from_high, (got_own[0], got_own[2])))
    from_low_b, from_high_b = other_core(from_low), other_core(from_high)
    cross = call(
        cross_lines_kernel, (packed,) * 5, [SMEM] * 4 + [ANY] * 4, (VMEM,) * 5,
        [pltpu.VMEM((2 * line_count * parts, LANES), F32), pltpu.SemaphoreType.DMA((4,))],
    )(*asked, from_low, from_low_b, from_high, from_high_b)
    got_cross = [along_x(cross[1 + step], step) for step in (1, 2, 3)]

    slot_ids = corners.reshape(4, line_count)
    offset = slot_ids // capacity - REACH
    source = here + offset
    outside = (source < 0) | (source >= RING)
    behind = (here - source) % RING
    held_at = jnp.where(
        behind == 0,
        jnp.where(offset == 0, 8, jnp.where(offset < 0, 3, 4)),
        behind + jnp.where(outside, -1, 4),
    )
    slot_ids = held_at * capacity + slot_ids % capacity
    flat_ids = slot_ids.reshape(1, 4 * line_count)
    blocks = got_cross + [cross[0], cross[1]] + got_own + [own[0]]
    here_part, ahead_part = call(
        weight_kernel, (f32s(4, line_count, cell_count),) * 2, [VMEM], (VMEM,) * 2,
    )(fractions.reshape(3, line_count, cell_count))
    half = f32s(row_count, cell_count)
    push_part = jax.ShapeDtypeStruct((4 * line_count, cell_count), BF16)
    warped_0, warped_1, push_high, push_low = call(
        warp_kernel,
        (half,) * 2 + (push_part,) * 2,
        [SMEM] + [VMEM] * 3 + [ANY] * 9,
        (VMEM,) * 4,
        [
            pltpu.VMEM((band_count * capacity * parts, LANES), F32),
            pltpu.VMEM((4 * WARP_ROWS * parts, LANES), F32),
            pltpu.VMEM((4 * WARP_ROWS * parts, LANES), F32),
            pltpu.SemaphoreType.DMA((9,)),
        ],
    )(slot_ids, here_part, ahead_part, images.reshape(line_count, cell_count), *blocks)

    block = f32s(capacity, cell_count)
    pool_cross = call(
        functools.partial(slot_sum_kernel, 0), (block,) * 5, [VMEM] * 3, (VMEM,) * 5,
    )(flat_ids, push_high, push_low)
    pool_own = call(
        functools.partial(slot_sum_kernel, 5), (block,) * 4, [VMEM] * 3, (VMEM,) * 4,
    )(flat_ids, push_high, push_low)
    back_cross = [along_x(pool_cross[step - 1], -step) for step in (1, 2, 3)]
    back_cross, pool_own = lax.optimization_barrier((back_cross, pool_own))
    back_own = [along_x(pool_own[step - 1], -step) for step in (1, 2, 3)]

    per_piece = row_count // (2 * RING)
    wide = per_piece + 2 * HALO
    at = jnp.arange(2 * RING * 2 * wide, dtype=I32)
    piece = at // (2 * wide)
    part = jnp.where(piece < RING, core, 1 - core)
    index = part * RING + (chip + piece) % RING
    row = index * per_piece - HALO + at % wide
    target = jnp.where((row >= 0) & (row < row_count), at // wide % 2 * row_count + row, -(2**20))
    target = target.reshape(-1, 1)
    core_part = f32s(RING * 2 * wide, cell_count)
    core_rows = core_part.shape[0]
    all_rows = 2 * core_rows
    hot_own, hot_low, hot_high = call(
        line_hot_kernel,
        (jax.ShapeDtypeStruct((all_rows, 4 * capacity), BF16),) + (jax.ShapeDtypeStruct((all_rows, 5 * capacity), BF16),) * 2,
        [SMEM] + [VMEM] * 5, (VMEM,) * 3,
    )(place, *asked, target)
    keep_low, keep_high, send = call(
        cross_back_kernel, (core_part,) * 2 + (f32s(2 * core_rows, cell_count),),
        [VMEM] * 7, (VMEM,) * 3,
    )(hot_low, hot_high, *pool_cross[3:], *back_cross)
    received = other_core(send)
    sum_low = keep_low + received[:core_rows]
    sum_high = keep_high + received[core_rows:]
    in_from_high = along_z(sum_low, -1)
    in_from_low = along_z(sum_high, 1)
    back_own, sum_low, sum_high = lax.optimization_barrier((back_own, sum_low, sum_high))
    size = 2 * wide
    keep_own, *send_own = call(
        own_back_kernel, (core_part,) + (f32s(core_rows // 2, cell_count),) * 2,
        [VMEM] * 5, (VMEM,) * 3,
    )(hot_own, pool_own[3], *back_own)
    got_parts = [other_core(part) for part in send_own]
    pieces = [
        keep_own[at * size:(at + 1) * size]
        + got_parts[at // 2][at % 2 * size:(at % 2 + 1) * size]
        + in_from_high[at * size:(at + 1) * size]
        + in_from_low[at * size:(at + 1) * size]
        for at in range(RING)
    ]
    piece_sum = pieces[0] + along_y(pieces[1], 1) + along_y(pieces[2], 2) + along_y(pieces[3], 3)
    edge_0, edge_1, _ = lax.optimization_barrier((warped_0, warped_1, piece_sum))
    edge_before, edge_after = along_slab(edge_1, 1), along_slab(edge_0, -1)
    before, after = along_slab(piece_sum, 1), along_slab(piece_sum, -1)
    new_piece = call(
        smooth_kernel, f32s(2 * per_piece, cell_count), [SMEM] + [VMEM] * 4, VMEM,
        [pltpu.VMEM((3 * size, cell_count), F32)],
    )(place, before, piece_sum, after, lines)

    image_lines = images.reshape(line_count, cell_count)
    force = f32s(3, plane_count, row_count, cell_count)
    part_force = call(
        plane_force_kernel, force, [VMEM] * 3, ANY,
        [pltpu.VMEM((2, plane_count, row_count, cell_count), F32), pltpu.SemaphoreType.DMA],
    )(warped_0, warped_1, image_lines)
    image_force = call(
        depth_force_kernel, force, [SMEM] + [VMEM] * 5 + [ANY], ANY,
        [pltpu.VMEM((1, plane_count, row_count, cell_count), F32), pltpu.SemaphoreType.DMA], {6: 0},
    )(place, edge_before, warped_0, warped_1, edge_after, image_lines, part_force)
    mine = [new_piece] + [along_y(new_piece, step) for step in (1, 2, 3)]
    theirs = [other_core(value) for value in mine]
    new_template = call(
        assemble_kernel, f32s(line_count, cell_count), [SMEM] + [ANY] * 8, ANY,
        [pltpu.SemaphoreType.DMA((16,))],
    )(place, *mine, *theirs)
    return new_template.reshape(template.shape), image_force[None]


def solution(mesh):
    return jax.shard_map(
        on_device,
        mesh=mesh,
        in_specs=(
            P("slab", None, None),
            P("subj", "slab", None, None),
            P("subj", None, "slab", None, None),
            P("subj", "slab", None, None),
            P("subj", None, "slab", None),
        ),
        out_specs=(P("slab", None, None), P("subj", None, "slab", None, None)),
        check_vma=False,
    )
```

```python
import functools

import jax
import jax.numpy as jnp
from jax import lax
from jax.experimental import pallas as pl
from jax.experimental.pallas import tpu as pltpu
from jax.sharding import PartitionSpec as P

SMOOTH = 2
REACH = 4
RING = 4
diffusion = 0.15
HALO = SMOOTH
LANES = 128
WARP_ROWS = 32

F32 = jnp.float32
BF16 = jnp.bfloat16
I32 = jnp.int32
VMEM = pl.BlockSpec(memory_space=pltpu.VMEM)
SMEM = pl.BlockSpec(memory_space=pltpu.SMEM)
ANY = pl.BlockSpec(memory_space=pl.ANY)
LIMIT = 8 * 2**20


def call(body, outs, in_specs, out_specs, scratch=(), aliases={}):
    return pl.pallas_call(
        body,
        out_shape=outs,
        in_specs=in_specs,
        out_specs=out_specs,
        scratch_shapes=list(scratch),
        input_output_aliases=aliases,
        compiler_params=pltpu.CompilerParams(vmem_limit_bytes=LIMIT),
    )


def f32s(*shape):
    return jax.ShapeDtypeStruct(shape, F32)


def along_x(value, step):
    count = lax.axis_size("slab")
    route = [(i, i // RING * RING + (i + step) % RING) for i in range(count)]
    return lax.ppermute(value, "slab", route)


def along_slab(value, step):
    count = lax.axis_size("slab")
    return lax.ppermute(value, "slab", [(i, (i + step) % count) for i in range(count)])


def along_z(value, step):
    return along_slab(value, RING * step)


def ring_of(move, values, sign):
    moved = {step: move(values[step - 1], sign * step) for step in (2, 1, 3)}
    return [moved[step] for step in (1, 2, 3)]


def other_core(value):
    count = lax.axis_size("subj")
    return lax.ppermute(value, "subj", [(i, i ^ 1) for i in range(count)])


def along_y(value, step):
    count = lax.axis_size("subj")
    return lax.ppermute(value, "subj", [(i, (i + 2 * step) % count) for i in range(count)])


def spread_rows(source_ref, out_ref):
    count, width = source_ref.shape
    parts = width // LANES

    def group(block, carry):
        first = pl.multiple_of(block * 8, 8)
        for part in range(parts):
            out_ref[pl.ds(first * parts + part, 8, stride=parts), :] = source_ref[
                pl.ds(first, 8), part * LANES:(part + 1) * LANES
            ]
        return carry

    lax.fori_loop(0, count // 8, group, 0, unroll=4)


def spread_plane_kernel(place_ref, source_ref, out_ref, held, sem):
    rows = held.shape[0]
    start = pl.multiple_of(place_ref[1] * rows, rows)
    copy = pltpu.make_async_copy(source_ref.at[pl.ds(start, rows)], held, sem)
    copy.start()
    copy.wait()
    spread_rows(held, out_ref)


def request_kernel(place_ref, lists_ref, self_ref, out_1, out_2, out_3):
    here = place_ref[0]
    line_count = place_ref[6]
    parts = place_ref[7]
    flip = place_ref[1] * (line_count // 2) * parts

    def across(row, above):
        return ((lists_ref[pl.ds(row, 1), :] * parts) ^ flip) + above * line_count * parts

    self_ref[0:1, :] = lists_ref[REACH:REACH + 1, :] * parts
    self_ref[1:2, :] = across(0, 0)
    self_ref[2:3, :] = across(2 * REACH, 1)
    for step, out in ((1, out_1), (2, out_2), (3, out_3)):
        server = lax.rem(here + RING - step, RING)
        above = (here > server).astype(I32)
        out[0:1, :] = lists_ref[pl.ds(server - here + REACH, 1), :] * parts
        out[1:2, :] = across(server - here + 2 * REACH * above, above)


def fill(held, parts):
    size = parts[0].shape[0]
    unit = 64
    for at, part in enumerate(parts):
        def group(block, carry):
            first = pl.multiple_of(block * unit, unit)
            held[pl.ds(at * size + first, unit), :] = part[pl.ds(first, unit), :]
            return carry

        lax.fori_loop(0, size // unit, group, 0, unroll=4)


def copy_lines(list_ref, list_row, held, out_ref):
    count = list_ref.shape[1]
    parts = out_ref.shape[0] // count
    unit = 16

    def group(block, carry):
        found = [
            held[pl.ds(pl.multiple_of(list_ref[list_row, block * unit + at], parts), parts), :] for at in range(unit)
        ]
        for at in range(unit):
            place = pl.multiple_of((block * unit + at) * parts, parts)
            out_ref[pl.ds(place, parts), :] = found[at]
        return carry

    lax.fori_loop(0, count // unit, group, 0, unroll=2)


def own_lines_kernel(lists_0, lists_1, lists_2, lists_3, held, out_0, out_1, out_2, out_3):
    for lists, out in ((lists_1, out_1), (lists_2, out_2), (lists_3, out_3), (lists_0, out_0)):
        copy_lines(lists, 0, held, out)


def cross_lines_kernel(
    lists_0, lists_1, lists_2, lists_3, low_a, low_b, high_a, high_b,
    out_low, out_high, out_1, out_2, out_3, held,
):
    fill(held, (low_a, low_b, high_a, high_b))
    for lists, row, out in (
        (lists_1, 1, out_1), (lists_2, 1, out_2), (lists_3, 1, out_3), (lists_0, 1, out_low), (lists_0, 2, out_high),
    ):
        copy_lines(lists, row, held, out)


def split_parts(value):
    high = value.astype(BF16)
    low = (value - high.astype(F32)).astype(BF16)
    return high, low


def shift_down(value):
    width = value.shape[1]
    lane = lax.broadcasted_iota(I32, value.shape, 1)
    return jnp.where(lane == width - 1, 0.0, pltpu.roll(value, width - 1, 1))


def shift_up(value):
    lane = lax.broadcasted_iota(I32, value.shape, 1)
    return jnp.where(lane == 0, 0.0, pltpu.roll(value, 1, 1))


def corner_parts(scale, depth_part, row_part):
    above, below = scale * depth_part, scale * (1.0 - depth_part)
    rest = 1.0 - row_part
    return below * rest, below * row_part, above * rest, above * row_part


def weight_kernel(fraction_ref, here_ref, ahead_ref):
    line_count, width = fraction_ref.shape[1:]
    rows = 16
    lane = lax.broadcasted_iota(I32, (rows, width), 1)

    def step(block, carry):
        first = pl.multiple_of(block * rows, rows)
        depth_part, row_part, across = [fraction_ref[at, pl.ds(first, rows), :].astype(F32) for at in range(3)]
        here = corner_parts(1.0 - across, depth_part, row_part)
        ahead = corner_parts(
            jnp.where(lane == 0, 0.0, pltpu.roll(across, 1, 1)),
            pltpu.roll(depth_part, 1, 1), pltpu.roll(row_part, 1, 1),
        )
        for corner in range(4):
            here_ref[corner, pl.ds(first, rows), :] = here[corner]
            ahead_ref[corner, pl.ds(first, rows), :] = ahead[corner]
        return carry

    lax.fori_loop(0, line_count // rows, step, 0)


def warp_kernel(*refs):
    slot_ref, here_ref, ahead_ref, image_ref = refs[:4]
    blocks = refs[4:13]
    warped_refs, push_high, push_low = refs[13:15], refs[15], refs[16]
    held, stage_0, stage_1 = refs[17:]
    line_count, width = image_ref.shape
    parts = width // LANES
    rows_plane = line_count // 2
    rows = WARP_ROWS
    fill(held, blocks)

    def gather(block, stage, corner, low, high):
        first = block * rows
        found = []
        for row in range(low, high):
            line = slot_ref[corner, first + row]
            found.append(held[pl.ds(pl.multiple_of(line, parts), parts), :])
        for row in range(low, high):
            at = (corner * rows + row) * parts
            stage[at:at + parts, :] = found[row - low]

    lane = lax.broadcasted_iota(I32, (rows, width), 1)

    def combine(plane, block, stage, following, stage_after):
        first = pl.multiple_of(block * rows, rows)
        near, far = None, None
        for corner in range(4):
            lines = jnp.concatenate(
                [stage[pl.ds(corner * rows * parts + part, rows, stride=parts), :] for part in range(parts)],
                axis=1,
            )
            near_term = here_ref[corner, pl.ds(first, rows), :] * lines
            far_term = ahead_ref[corner, pl.ds(first, rows), :] * lines
            gather(following, stage_after, corner, 0, rows // 2)
            near = near_term if near is None else near + near_term
            far = far_term if far is None else far + far_term
        warped = near + jnp.where(lane == width - 1, 0.0, pltpu.roll(far, width - 1, 1))
        warped_refs[plane][pl.ds(pl.multiple_of(first - plane * rows_plane, rows), rows), :] = warped
        mismatch = warped - image_ref[pl.ds(first, rows), :]
        behind = pltpu.roll(mismatch, 1, 1)
        for corner in range(4):
            here, ahead = here_ref[corner, pl.ds(first, rows), :], ahead_ref[corner, pl.ds(first, rows), :]
            high, low = split_parts(here * mismatch + ahead * behind)
            gather(following, stage_after, corner, rows // 2, rows)
            at = pl.multiple_of(corner * line_count + first, rows)
            push_high[pl.ds(at, rows), :] = high
            push_low[pl.ds(at, rows), :] = low

    blocks_plane = rows_plane // rows
    last = 2 * blocks_plane - 1
    for corner in range(4):
        gather(0, stage_0, corner, 0, rows)
    for plane in range(2):
        def step(pair, carry):
            block = plane * blocks_plane + 2 * pair
            combine(plane, block, stage_0, block + 1, stage_1)
            combine(plane, block + 1, stage_1, jnp.minimum(block + 2, last), stage_0)
            return carry

        lax.fori_loop(0, blocks_plane // 2, step, 0)


def slot_sum_kernel(first, ids_ref, push_high, push_low, *outs):
    capacity = outs[0].shape[0]
    slot = lax.broadcasted_iota(I32, (capacity, push_high.shape[0]), 0)
    for start in range(0, len(outs), 3):
        chosen = outs[start:start + 3]
        hot = jnp.concatenate(
            [
                jnp.where(ids_ref[...] == slot + (first + start + at) * capacity, 1.0, 0.0).astype(BF16)
                for at in range(len(chosen))
            ],
            axis=0,
        )
        summed = jnp.dot(hot, push_high[...], preferred_element_type=F32)
        summed = summed + jnp.dot(hot, push_low[...], preferred_element_type=F32)
        for at, out in enumerate(chosen):
            out[...] = summed[at * capacity:(at + 1) * capacity]


def line_hot_kernel(place_ref, lists_0, lists_1, lists_2, lists_3, rows_ref, own_ref, low_ref, high_ref):
    capacity = lists_0.shape[1]
    line_count, parts = place_ref[6], place_ref[7]
    flip = place_ref[1] * (line_count // 2) * parts
    rows = rows_ref[...] * parts

    def hot(ids):
        return jnp.where(rows == ids, 1.0, 0.0).astype(BF16)

    own_lists = (lists_0[0:1, :], lists_1[0:1, :], lists_2[0:1, :], lists_3[0:1, :])
    cross_lists = (lists_0[1:2, :], lists_0[2:3, :], lists_1[1:2, :], lists_2[1:2, :], lists_3[1:2, :])
    for at, ids in enumerate(own_lists + own_lists):
        own_ref[:, at * capacity:(at + 1) * capacity] = hot(ids)
    for at, ids in enumerate(cross_lists + cross_lists):
        ids = ids ^ flip
        low_ref[:, at * capacity:(at + 1) * capacity] = hot(ids)
        high_ref[:, at * capacity:(at + 1) * capacity] = hot(ids - line_count * parts)


def stacked_parts(blocks):
    return jnp.concatenate(split_parts(jnp.concatenate([block[...] for block in blocks], axis=0)), axis=0)


def own_back_kernel(hot_ref, in_0, in_1, in_2, in_3, keep, send_0, send_1):
    summed = jnp.dot(hot_ref[...], stacked_parts((in_0, in_1, in_2, in_3)), preferred_element_type=F32)
    count, first = keep.shape[0], send_0.shape[0]
    keep[...] = summed[:count]
    send_0[...] = summed[count:count + first]
    send_1[...] = summed[count + first:]


def cross_back_kernel(hot_low, hot_high, in_low, in_high, in_1, in_2, in_3, keep_low, keep_high, send):
    values = stacked_parts((in_low, in_high, in_1, in_2, in_3))
    count = keep_low.shape[0]
    for at, (hot, keep) in enumerate(((hot_low, keep_low), (hot_high, keep_high))):
        summed = jnp.dot(hot[...], values, preferred_element_type=F32)
        keep[...] = summed[:count]
        send[at * count:(at + 1) * count] = summed[count:]


def smooth_kernel(place_ref, before, piece, after, template_ref, out, field):
    device, last, core, chip = place_ref[2], place_ref[3], place_ref[1], place_ref[4]
    size = piece.shape[0]
    rows = size // 2
    total = 3 * size
    zero = jnp.zeros(piece.shape, F32)
    field[0:size, :] = jnp.where(device > 0, before[...], zero)
    field[size:2 * size, :] = piece[...]
    field[2 * size:3 * size, :] = jnp.where(device < last, after[...], zero)
    width = piece.shape[1]
    at = lax.broadcasted_iota(I32, (total, width), 0)
    row = lax.rem(at, rows)
    per_piece = rows - 2 * HALO
    index = core * RING + chip
    row = row + index * per_piece - HALO
    inside = (row >= 0) & (row < 2 * RING * per_piece)
    inside = inside & ((at >= size) | (device > 0)) & ((at < 2 * size) | (device < last))
    current = field[...]
    for repeat in range(SMOOTH):
        beside = pltpu.roll(current, rows, 0) + pltpu.roll(current, total - rows, 0)
        beside = beside + pltpu.roll(current, 1, 0) + pltpu.roll(current, total - 1, 0)
        beside = beside + shift_up(current) + shift_down(current)
        current = current + diffusion * (beside - 6.0 * current)
        if repeat < SMOOTH - 1:
            current = jnp.where(inside, current, 0.0)
    field[...] = current
    subjects = place_ref[5].astype(F32)
    plane_rows = template_ref.shape[0] // 2
    for plane in range(2):
        start = pl.multiple_of(plane * plane_rows + index * per_piece, per_piece)
        found = field[pl.ds(size + plane * rows + HALO, per_piece), :]
        out[plane * per_piece:(plane + 1) * per_piece, :] = (
            template_ref[pl.ds(start, per_piece), :] - found / subjects
        )


def plane_force_kernel(plane_0, plane_1, image_ref, out, held, sem):
    rows_plane, width = plane_0.shape
    rows = 32
    row = lax.broadcasted_iota(I32, (rows, width), 0)
    for plane, current in enumerate((plane_0, plane_1)):
        def step(block, carry):
            first = pl.multiple_of(block * rows, rows)
            centre = current[pl.ds(first, rows), :]
            negative = image_ref[pl.ds(plane * rows_plane + first, rows), :] - centre
            above = current[pl.ds(jnp.maximum(first - 1, 0), 1), :]
            above = jnp.where(first > 0, above, 0.0)
            below = current[pl.ds(jnp.minimum(first + rows, rows_plane - 1), 1), :]
            below = jnp.where(first + rows < rows_plane, below, 0.0)
            up = jnp.where(row == 0, above, pltpu.roll(centre, 1, 0))
            down = jnp.where(row == rows - 1, below, pltpu.roll(centre, rows - 1, 0))
            held[0, plane, pl.ds(first, rows), :] = negative * (0.5 * (down - up))
            held[1, plane, pl.ds(first, rows), :] = negative * (0.5 * (shift_down(centre) - shift_up(centre)))
            return carry

        lax.fori_loop(0, rows_plane // rows, step, 0)
    copy = pltpu.make_async_copy(held, out.at[pl.ds(1, 2)], sem)
    copy.start()
    copy.wait()


def finish_kernel(place_ref, before, plane_0, plane_1, after, image_ref, *refs):
    pieces = refs[:2 * RING]
    template_out, out, held, sems = refs[2 * RING + 1:]
    device, last, core, chip = place_ref[2], place_ref[3], place_ref[1], place_ref[4]
    count = pieces[0].shape[0] // 2
    rows_plane = plane_0.shape[0]
    copies = []
    for at, piece in enumerate(pieces):
        part = core if at < RING else 1 - core
        index = part * RING + lax.rem(chip + RING - at % RING, RING)
        for plane in range(2):
            start = pl.multiple_of(plane * rows_plane + index * count, count)
            copies.append(
                pltpu.make_async_copy(
                    piece.at[pl.ds(plane * count, count)], template_out.at[pl.ds(start, count)], sems.at[2 * at + plane]
                )
            )
    for copy in copies:
        copy.start()
    rows = 32
    for plane in range(2):
        def step(block, carry):
            at = pl.ds(pl.multiple_of(block * rows, rows), rows)
            image = image_ref[pl.ds(pl.multiple_of(plane * rows_plane + block * rows, rows), rows), :]
            if plane == 0:
                centre, back, ahead = plane_0[at, :], jnp.where(device > 0, before[at, :], 0.0), plane_1[at, :]
            else:
                centre, back, ahead = plane_1[at, :], plane_0[at, :], jnp.where(device < last, after[at, :], 0.0)
            held[plane, at, :] = (image - centre) * (0.5 * (ahead - back))
            return carry

        lax.fori_loop(0, rows_plane // rows, step, 0)
        copy = pltpu.make_async_copy(held.at[plane], out.at[0, plane], sems.at[4 * RING + plane])
        copy.start()
        copies.append(copy)
    for copy in copies:
        copy.wait()


def on_device(template, images, fractions, requests, corners):
    _, plane_count, row_count, cell_count = images.shape
    line_count = plane_count * row_count
    band_count, capacity = requests.shape[2:]
    slab = lax.axis_index("slab")
    subject = lax.axis_index("subj")
    last = lax.axis_size("slab") - 1
    here = slab % RING
    core = subject % 2
    chip = subject // 2
    fixed = [last, lax.axis_size("subj"), line_count, cell_count // LANES]
    place = jnp.stack([here, core, slab, fixed[0], chip, fixed[1], fixed[2], fixed[3]]).astype(I32)
    lists = requests.reshape(band_count, capacity)
    lines = template.reshape(line_count, cell_count)
    parts = cell_count // LANES
    packed = f32s(capacity * parts, LANES)

    message = jax.ShapeDtypeStruct((2, capacity), I32)
    self_lists, *messages = call(
        request_kernel, (jax.ShapeDtypeStruct((3, capacity), I32),) + (message,) * 3, [SMEM, VMEM], (VMEM,) * 4,
    )(place, lists)
    plane = call(
        spread_plane_kernel, f32s(row_count * parts, LANES), [SMEM, ANY], VMEM,
        [pltpu.VMEM((row_count, cell_count), F32), pltpu.SemaphoreType.DMA],
    )(place, lines)
    spread = call(spread_rows, f32s(line_count * parts, LANES), [VMEM], VMEM)(lines)
    from_low = along_z(plane, 1)
    from_high = along_z(plane, -1)
    asked = [self_lists] + ring_of(along_x, messages, -1)

    own = call(
        own_lines_kernel, (packed,) * 4, [SMEM] * 4 + [VMEM], (VMEM,) * 4,
    )(*asked, spread)
    got_own = ring_of(along_x, own[1:], 1)
    from_low, from_high, _ = lax.optimization_barrier((from_low, from_high, (got_own[0], got_own[2])))
    from_low_b, from_high_b = other_core(from_low), other_core(from_high)
    cross = call(
        cross_lines_kernel, (packed,) * 5, [SMEM] * 4 + [VMEM] * 4, (VMEM,) * 5,
        [pltpu.VMEM((2 * line_count * parts, LANES), F32)],
    )(*asked, from_low, from_low_b, from_high, from_high_b)
    got_cross = ring_of(along_x, cross[2:], 1)

    slot_ids = corners.reshape(4, line_count)
    offset = slot_ids // capacity - REACH
    source = here + offset
    outside = (source < 0) | (source >= RING)
    behind = (here - source) % RING
    held_at = jnp.where(
        behind == 0,
        jnp.where(offset == 0, 8, jnp.where(offset < 0, 3, 4)),
        behind + jnp.where(outside, -1, 4),
    )
    slot_ids = held_at * capacity + slot_ids % capacity
    flat_ids = slot_ids.reshape(1, 4 * line_count)
    blocks = got_cross + [cross[0], cross[1]] + got_own + [own[0]]
    here_part, ahead_part = call(
        weight_kernel, (f32s(4, line_count, cell_count),) * 2, [VMEM], (VMEM,) * 2,
    )(fractions.reshape(3, line_count, cell_count))
    half = f32s(row_count, cell_count)
    push_part = jax.ShapeDtypeStruct((4 * line_count, cell_count), BF16)
    warped_0, warped_1, push_high, push_low = call(
        warp_kernel,
        (half,) * 2 + (push_part,) * 2,
        [SMEM] + [VMEM] * 12,
        (VMEM,) * 4,
        [
            pltpu.VMEM((band_count * capacity * parts, LANES), F32),
            pltpu.VMEM((4 * WARP_ROWS * parts, LANES), F32),
            pltpu.VMEM((4 * WARP_ROWS * parts, LANES), F32),
        ],
    )(slot_ids * parts, here_part, ahead_part, images.reshape(line_count, cell_count), *blocks)

    block = f32s(capacity, cell_count)
    pool_cross = call(
        functools.partial(slot_sum_kernel, 0), (block,) * 3, [VMEM] * 3, (VMEM,) * 3,
    )(flat_ids, push_high, push_low)
    pool_low, pool_high, *pool_own = call(
        functools.partial(slot_sum_kernel, 3), (block,) * 6, [VMEM] * 3, (VMEM,) * 6,
    )(flat_ids, push_high, push_low)
    back_cross = ring_of(along_x, pool_cross, -1)
    image_lines = images.reshape(line_count, cell_count)
    force = f32s(3, plane_count, row_count, cell_count)
    part_force = call(
        plane_force_kernel, force, [VMEM] * 3, ANY,
        [pltpu.VMEM((2, plane_count, row_count, cell_count), F32), pltpu.SemaphoreType.DMA],
    )(warped_0, warped_1, image_lines)
    back_cross, pool_own, part_force = lax.optimization_barrier((back_cross, pool_own, part_force))
    back_own = ring_of(along_x, pool_own, -1)

    per_piece = row_count // (2 * RING)
    wide = per_piece + 2 * HALO
    at = jnp.arange(2 * RING * 2 * wide, dtype=I32)
    piece = at // (2 * wide)
    part = jnp.where(piece < RING, core, 1 - core)
    index = part * RING + (chip + piece) % RING
    row = index * per_piece - HALO + at % wide
    target = jnp.where((row >= 0) & (row < row_count), at // wide % 2 * row_count + row, -(2**20))
    target = target.reshape(-1, 1)
    core_part = f32s(RING * 2 * wide, cell_count)
    core_rows = core_part.shape[0]
    all_rows = 2 * core_rows
    hot_own, hot_low, hot_high = call(
        line_hot_kernel,
        (jax.ShapeDtypeStruct((all_rows, 8 * capacity), BF16),) + (jax.ShapeDtypeStruct((all_rows, 10 * capacity), BF16),) * 2,
        [SMEM] + [VMEM] * 5, (VMEM,) * 3,
    )(place, *asked, target)
    keep_low, keep_high, send = call(
        cross_back_kernel, (core_part,) * 2 + (f32s(2 * core_rows, cell_count),),
        [VMEM] * 7, (VMEM,) * 3,
    )(hot_low, hot_high, pool_low, pool_high, *back_cross)
    received = other_core(send)
    sum_low = keep_low + received[:core_rows]
    sum_high = keep_high + received[core_rows:]
    in_from_high = along_z(sum_low, -1)
    in_from_low = along_z(sum_high, 1)
    back_own, sum_low, sum_high = lax.optimization_barrier((back_own, sum_low, sum_high))
    size = 2 * wide
    keep_own, *send_own = call(
        own_back_kernel, (core_part, f32s(core_rows - size, cell_count), f32s(size, cell_count)),
        [VMEM] * 5, (VMEM,) * 3,
    )(hot_own, pool_own[3], *back_own)
    got_parts = [other_core(part) for part in send_own]
    pieces = [
        keep_own[at * size:(at + 1) * size]
        + (got_parts[0][at * size:(at + 1) * size] if at < RING - 1 else got_parts[1])
        + in_from_high[at * size:(at + 1) * size]
        + in_from_low[at * size:(at + 1) * size]
        for at in range(RING)
    ]
    got_pieces = ring_of(along_y, pieces[1:], 1)
    piece_sum = pieces[0] + got_pieces[0] + got_pieces[1] + got_pieces[2]
    edge_0, edge_1, _ = lax.optimization_barrier((warped_0, warped_1, piece_sum))
    edge_before, edge_after = along_slab(edge_1, 1), along_slab(edge_0, -1)
    before, after = along_slab(piece_sum, 1), along_slab(piece_sum, -1)
    new_piece = call(
        smooth_kernel, f32s(2 * per_piece, cell_count), [SMEM] + [VMEM] * 4, VMEM,
        [pltpu.VMEM((3 * size, cell_count), F32)],
    )(place, before, piece_sum, after, lines)

    mine = [new_piece] + ring_of(along_y, [new_piece] * 3, 1)
    theirs = [other_core(value) for value in mine]
    new_template, image_force = call(
        finish_kernel, (f32s(line_count, cell_count), force), [SMEM] + [VMEM] * 5 + [ANY] * 9, (ANY, ANY),
        [pltpu.VMEM((plane_count, row_count, cell_count), F32), pltpu.SemaphoreType.DMA((4 * RING + 2,))],
        {14: 1},
    )(place, edge_before, warped_0, warped_1, edge_after, image_lines, *mine, *theirs, part_force)
    return new_template.reshape(template.shape), image_force[None]


def solution(mesh):
    return jax.shard_map(
        on_device,
        mesh=mesh,
        in_specs=(
            P("slab", None, None),
            P("subj", "slab", None, None),
            P("subj", None, "slab", None, None),
            P("subj", "slab", None, None),
            P("subj", None, "slab", None),
        ),
        out_specs=(P("slab", None, None), P("subj", None, "slab", None, None)),
        check_vma=False,
    )
```

```python
import functools

import jax
import jax.numpy as jnp
from jax import lax
from jax.experimental import pallas as pl
from jax.experimental.pallas import tpu as pltpu
from jax.sharding import PartitionSpec as P

SMOOTH = 2
REACH = 4
RING = 4
diffusion = 0.15
HALO = SMOOTH
LANES = 128
WARP_ROWS = 32

F32 = jnp.float32
BF16 = jnp.bfloat16
I32 = jnp.int32
VMEM = pl.BlockSpec(memory_space=pltpu.VMEM)
SMEM = pl.BlockSpec(memory_space=pltpu.SMEM)
ANY = pl.BlockSpec(memory_space=pl.ANY)
LIMIT = 8 * 2**20


def call(body, outs, in_specs, out_specs, scratch=(), aliases={}):
    return pl.pallas_call(
        body,
        out_shape=outs,
        in_specs=in_specs,
        out_specs=out_specs,
        scratch_shapes=list(scratch),
        input_output_aliases=aliases,
        compiler_params=pltpu.CompilerParams(vmem_limit_bytes=LIMIT),
    )


def f32s(*shape):
    return jax.ShapeDtypeStruct(shape, F32)


def along_x(value, step):
    count = lax.axis_size("slab")
    route = [(i, i // RING * RING + (i + step) % RING) for i in range(count)]
    return lax.ppermute(value, "slab", route)


def along_slab(value, step):
    count = lax.axis_size("slab")
    return lax.ppermute(value, "slab", [(i, (i + step) % count) for i in range(count)])


def along_z(value, step):
    return along_slab(value, RING * step)


def ring_of(move, values, sign):
    moved = {step: move(values[step - 1], sign * step) for step in (2, 1, 3)}
    return [moved[step] for step in (1, 2, 3)]


def other_core(value):
    count = lax.axis_size("subj")
    return lax.ppermute(value, "subj", [(i, i ^ 1) for i in range(count)])


def along_y(value, step):
    count = lax.axis_size("subj")
    return lax.ppermute(value, "subj", [(i, (i + 2 * step) % count) for i in range(count)])


def spread_rows(source_ref, start, count, out_ref):
    parts = source_ref.shape[1] // LANES

    def group(block, carry):
        first = pl.multiple_of(block * 8, 8)
        for part in range(parts):
            out_ref[pl.ds(first * parts + part, 8, stride=parts), :] = source_ref[
                pl.ds(pl.multiple_of(start + first, 8), 8), part * LANES:(part + 1) * LANES
            ]
        return carry

    lax.fori_loop(0, count // 8, group, 0, unroll=4)


def spread_plane_kernel(place_ref, source_ref, out_ref):
    rows = source_ref.shape[0] // 2
    spread_rows(source_ref, place_ref[1] * rows, rows, out_ref)


def spread_kernel(source_ref, out_ref):
    spread_rows(source_ref, 0, source_ref.shape[0], out_ref)


def request_kernel(place_ref, lists_ref, self_ref, out_1, out_2, out_3):
    here = place_ref[0]
    line_count = place_ref[6]
    parts = place_ref[7]
    flip = place_ref[1] * (line_count // 2) * parts

    def across(row, above):
        return ((lists_ref[pl.ds(row, 1), :] * parts) ^ flip) + above * line_count * parts

    self_ref[0:1, :] = lists_ref[REACH:REACH + 1, :] * parts
    self_ref[1:2, :] = across(0, 0)
    self_ref[2:3, :] = across(2 * REACH, 1)
    for step, out in ((1, out_1), (2, out_2), (3, out_3)):
        server = lax.rem(here + RING - step, RING)
        above = (here > server).astype(I32)
        out[0:1, :] = lists_ref[pl.ds(server - here + REACH, 1), :] * parts
        out[1:2, :] = across(server - here + 2 * REACH * above, above)


def fill(held, parts):
    size = parts[0].shape[0]
    unit = 64
    for at, part in enumerate(parts):
        def group(block, carry):
            first = pl.multiple_of(block * unit, unit)
            held[pl.ds(at * size + first, unit), :] = part[pl.ds(first, unit), :]
            return carry

        lax.fori_loop(0, size // unit, group, 0, unroll=4)


def copy_lines(list_ref, list_row, held, out_ref):
    count = list_ref.shape[1]
    parts = out_ref.shape[0] // count
    unit = 16

    def group(block, carry):
        found = [
            held[pl.ds(pl.multiple_of(list_ref[list_row, block * unit + at], parts), parts), :] for at in range(unit)
        ]
        for at in range(unit):
            place = pl.multiple_of((block * unit + at) * parts, parts)
            out_ref[pl.ds(place, parts), :] = found[at]
        return carry

    lax.fori_loop(0, count // unit, group, 0, unroll=2)


def own_lines_kernel(lists_1, lists_2, lists_3, held, out_1, out_2, out_3):
    for lists, out in ((lists_1, out_1), (lists_2, out_2), (lists_3, out_3)):
        copy_lines(lists, 0, held, out)


def cross_lines_kernel(lists_1, lists_2, lists_3, low_a, low_b, high_a, high_b, out_1, out_2, out_3, held):
    fill(held, (low_a, low_b, high_a, high_b))
    for lists, out in ((lists_1, out_1), (lists_2, out_2), (lists_3, out_3)):
        copy_lines(lists, 1, held, out)


def self_lines_kernel(lists, own, low_a, low_b, high_a, high_b, out_low, out_high, out_own, held):
    fill(held, (low_a, low_b, high_a, high_b))
    copy_lines(lists, 0, own, out_own)
    copy_lines(lists, 1, held, out_low)
    copy_lines(lists, 2, held, out_high)


def split_parts(value):
    high = value.astype(BF16)
    low = (value - high.astype(F32)).astype(BF16)
    return high, low


def shift_down(value):
    width = value.shape[1]
    lane = lax.broadcasted_iota(I32, value.shape, 1)
    return jnp.where(lane == width - 1, 0.0, pltpu.roll(value, width - 1, 1))


def shift_up(value):
    lane = lax.broadcasted_iota(I32, value.shape, 1)
    return jnp.where(lane == 0, 0.0, pltpu.roll(value, 1, 1))


def corner_parts(scale, depth_part, row_part):
    above, below = scale * depth_part, scale * (1.0 - depth_part)
    rest = 1.0 - row_part
    return below * rest, below * row_part, above * rest, above * row_part


def weight_kernel(fraction_ref, here_ref, ahead_ref):
    line_count, width = fraction_ref.shape[1:]
    rows = 16
    lane = lax.broadcasted_iota(I32, (rows, width), 1)

    def step(block, carry):
        first = pl.multiple_of(block * rows, rows)
        depth_part, row_part, across = [fraction_ref[at, pl.ds(first, rows), :].astype(F32) for at in range(3)]
        here = corner_parts(1.0 - across, depth_part, row_part)
        ahead = corner_parts(
            jnp.where(lane == 0, 0.0, pltpu.roll(across, 1, 1)),
            pltpu.roll(depth_part, 1, 1), pltpu.roll(row_part, 1, 1),
        )
        for corner in range(4):
            here_ref[corner, pl.ds(first, rows), :] = here[corner]
            ahead_ref[corner, pl.ds(first, rows), :] = ahead[corner]
        return carry

    lax.fori_loop(0, line_count // rows, step, 0)


def warp_kernel(*refs):
    slot_ref, here_ref, ahead_ref, image_ref = refs[:4]
    blocks = refs[4:13]
    warped_refs, push_high, push_low = refs[13:15], refs[15], refs[16]
    held, stage_0, stage_1 = refs[17:]
    line_count, width = image_ref.shape
    parts = width // LANES
    rows_plane = line_count // 2
    rows = WARP_ROWS
    fill(held, blocks)

    def gather(block, stage, corner, low, high):
        first = block * rows
        found = []
        for row in range(low, high):
            line = slot_ref[corner, first + row]
            found.append(held[pl.ds(pl.multiple_of(line, parts), parts), :])
        for row in range(low, high):
            at = (corner * rows + row) * parts
            stage[at:at + parts, :] = found[row - low]

    lane = lax.broadcasted_iota(I32, (rows, width), 1)

    def combine(plane, block, stage, following, stage_after):
        first = pl.multiple_of(block * rows, rows)
        near, far = None, None
        for corner in range(4):
            lines = jnp.concatenate(
                [stage[pl.ds(corner * rows * parts + part, rows, stride=parts), :] for part in range(parts)],
                axis=1,
            )
            near_term = here_ref[corner, pl.ds(first, rows), :] * lines
            far_term = ahead_ref[corner, pl.ds(first, rows), :] * lines
            gather(following, stage_after, corner, 0, rows // 2)
            near = near_term if near is None else near + near_term
            far = far_term if far is None else far + far_term
        warped = near + jnp.where(lane == width - 1, 0.0, pltpu.roll(far, width - 1, 1))
        warped_refs[plane][pl.ds(pl.multiple_of(first - plane * rows_plane, rows), rows), :] = warped
        mismatch = warped - image_ref[pl.ds(first, rows), :]
        behind = pltpu.roll(mismatch, 1, 1)
        for corner in range(4):
            here, ahead = here_ref[corner, pl.ds(first, rows), :], ahead_ref[corner, pl.ds(first, rows), :]
            high, low = split_parts(here * mismatch + ahead * behind)
            gather(following, stage_after, corner, rows // 2, rows)
            at = pl.multiple_of(corner * line_count + first, rows)
            push_high[pl.ds(at, rows), :] = high
            push_low[pl.ds(at, rows), :] = low

    blocks_plane = rows_plane // rows
    last = 2 * blocks_plane - 1
    for corner in range(4):
        gather(0, stage_0, corner, 0, rows)
    for plane in range(2):
        def step(pair, carry):
            block = plane * blocks_plane + 2 * pair
            combine(plane, block, stage_0, block + 1, stage_1)
            combine(plane, block + 1, stage_1, jnp.minimum(block + 2, last), stage_0)
            return carry

        lax.fori_loop(0, blocks_plane // 2, step, 0)


def slot_sum_kernel(first, ids_ref, push_high, push_low, *outs):
    capacity = outs[0].shape[0]
    slot = lax.broadcasted_iota(I32, (capacity, push_high.shape[0]), 0)
    for start in range(0, len(outs), 3):
        chosen = outs[start:start + 3]
        hot = jnp.concatenate(
            [
                jnp.where(ids_ref[...] == slot + (first + start + at) * capacity, 1.0, 0.0).astype(BF16)
                for at in range(len(chosen))
            ],
            axis=0,
        )
        summed = jnp.dot(hot, push_high[...], preferred_element_type=F32)
        summed = summed + jnp.dot(hot, push_low[...], preferred_element_type=F32)
        for at, out in enumerate(chosen):
            out[...] = summed[at * capacity:(at + 1) * capacity]


def line_hot_kernel(place_ref, lists_0, lists_1, lists_2, lists_3, rows_ref, own_ref, low_ref, high_ref):
    capacity = lists_0.shape[1]
    line_count, parts = place_ref[6], place_ref[7]
    flip = place_ref[1] * (line_count // 2) * parts
    rows = rows_ref[...] * parts

    def hot(ids):
        return jnp.where(rows == ids, 1.0, 0.0).astype(BF16)

    own_lists = (lists_0[0:1, :], lists_1[0:1, :], lists_2[0:1, :], lists_3[0:1, :])
    cross_lists = (lists_0[1:2, :], lists_0[2:3, :], lists_1[1:2, :], lists_2[1:2, :], lists_3[1:2, :])
    for at, ids in enumerate(own_lists + own_lists):
        own_ref[:, at * capacity:(at + 1) * capacity] = hot(ids)
    for at, ids in enumerate(cross_lists + cross_lists):
        ids = ids ^ flip
        low_ref[:, at * capacity:(at + 1) * capacity] = hot(ids)
        high_ref[:, at * capacity:(at + 1) * capacity] = hot(ids - line_count * parts)


def stacked_parts(blocks):
    return jnp.concatenate(split_parts(jnp.concatenate([block[...] for block in blocks], axis=0)), axis=0)


def own_back_kernel(hot_ref, in_0, in_1, in_2, in_3, keep, send_0, send_1):
    summed = jnp.dot(hot_ref[...], stacked_parts((in_0, in_1, in_2, in_3)), preferred_element_type=F32)
    count, first = keep.shape[0], send_0.shape[0]
    keep[...] = summed[:count]
    send_0[...] = summed[count:count + first]
    send_1[...] = summed[count + first:]


def cross_back_kernel(hot_low, hot_high, in_low, in_high, in_1, in_2, in_3, keep_low, keep_high, send):
    values = stacked_parts((in_low, in_high, in_1, in_2, in_3))
    count = keep_low.shape[0]
    for at, (hot, keep) in enumerate(((hot_low, keep_low), (hot_high, keep_high))):
        summed = jnp.dot(hot[...], values, preferred_element_type=F32)
        keep[...] = summed[:count]
        send[at * count:(at + 1) * count] = summed[count:]


def smooth_kernel(place_ref, before, piece, after, template_ref, out, field):
    device, last, core, chip = place_ref[2], place_ref[3], place_ref[1], place_ref[4]
    size = piece.shape[0]
    rows = size // 2
    total = 3 * size
    zero = jnp.zeros(piece.shape, F32)
    field[0:size, :] = jnp.where(device > 0, before[...], zero)
    field[size:2 * size, :] = piece[...]
    field[2 * size:3 * size, :] = jnp.where(device < last, after[...], zero)
    width = piece.shape[1]
    at = lax.broadcasted_iota(I32, (total, width), 0)
    row = lax.rem(at, rows)
    per_piece = rows - 2 * HALO
    index = core * RING + chip
    row = row + index * per_piece - HALO
    inside = (row >= 0) & (row < 2 * RING * per_piece)
    inside = inside & ((at >= size) | (device > 0)) & ((at < 2 * size) | (device < last))
    current = field[...]
    for repeat in range(SMOOTH):
        beside = pltpu.roll(current, rows, 0) + pltpu.roll(current, total - rows, 0)
        beside = beside + pltpu.roll(current, 1, 0) + pltpu.roll(current, total - 1, 0)
        beside = beside + shift_up(current) + shift_down(current)
        current = current + diffusion * (beside - 6.0 * current)
        if repeat < SMOOTH - 1:
            current = jnp.where(inside, current, 0.0)
    field[...] = current
    subjects = place_ref[5].astype(F32)
    plane_rows = template_ref.shape[0] // 2
    for plane in range(2):
        start = pl.multiple_of(plane * plane_rows + index * per_piece, per_piece)
        found = field[pl.ds(size + plane * rows + HALO, per_piece), :]
        out[plane * per_piece:(plane + 1) * per_piece, :] = (
            template_ref[pl.ds(start, per_piece), :] - found / subjects
        )


def plane_force_kernel(plane_0, plane_1, image_ref, out, held, sem):
    rows_plane, width = plane_0.shape
    rows = 32
    row = lax.broadcasted_iota(I32, (rows, width), 0)
    for plane, current in enumerate((plane_0, plane_1)):
        def step(block, carry):
            first = pl.multiple_of(block * rows, rows)
            centre = current[pl.ds(first, rows), :]
            negative = image_ref[pl.ds(plane * rows_plane + first, rows), :] - centre
            above = current[pl.ds(jnp.maximum(first - 1, 0), 1), :]
            above = jnp.where(first > 0, above, 0.0)
            below = current[pl.ds(jnp.minimum(first + rows, rows_plane - 1), 1), :]
            below = jnp.where(first + rows < rows_plane, below, 0.0)
            up = jnp.where(row == 0, above, pltpu.roll(centre, 1, 0))
            down = jnp.where(row == rows - 1, below, pltpu.roll(centre, rows - 1, 0))
            held[0, plane, pl.ds(first, rows), :] = negative * (0.5 * (down - up))
            held[1, plane, pl.ds(first, rows), :] = negative * (0.5 * (shift_down(centre) - shift_up(centre)))
            return carry

        lax.fori_loop(0, rows_plane // rows, step, 0)
    copy = pltpu.make_async_copy(held, out.at[pl.ds(1, 2)], sem)
    copy.start()
    copy.wait()


def finish_kernel(place_ref, before, plane_0, plane_1, after, image_ref, *refs):
    pieces = refs[:2 * RING]
    template_out, out, held, sems = refs[2 * RING + 1:]
    device, last, core, chip = place_ref[2], place_ref[3], place_ref[1], place_ref[4]
    count = pieces[0].shape[0] // 2
    rows_plane = plane_0.shape[0]
    copies = []
    for at, piece in enumerate(pieces):
        part = core if at < RING else 1 - core
        index = part * RING + lax.rem(chip + RING - at % RING, RING)
        for plane in range(2):
            start = pl.multiple_of(plane * rows_plane + index * count, count)
            copies.append(
                pltpu.make_async_copy(
                    piece.at[pl.ds(plane * count, count)], template_out.at[pl.ds(start, count)], sems.at[2 * at + plane]
                )
            )
    for copy in copies:
        copy.start()
    rows = 32
    for plane in range(2):
        def step(block, carry):
            at = pl.ds(pl.multiple_of(block * rows, rows), rows)
            image = image_ref[pl.ds(pl.multiple_of(plane * rows_plane + block * rows, rows), rows), :]
            if plane == 0:
                centre, back, ahead = plane_0[at, :], jnp.where(device > 0, before[at, :], 0.0), plane_1[at, :]
            else:
                centre, back, ahead = plane_1[at, :], plane_0[at, :], jnp.where(device < last, after[at, :], 0.0)
            held[plane, at, :] = (image - centre) * (0.5 * (ahead - back))
            return carry

        lax.fori_loop(0, rows_plane // rows, step, 0)
        copy = pltpu.make_async_copy(held.at[plane], out.at[0, plane], sems.at[4 * RING + plane])
        copy.start()
        copies.append(copy)
    for copy in copies:
        copy.wait()


def on_device(template, images, fractions, requests, corners):
    _, plane_count, row_count, cell_count = images.shape
    line_count = plane_count * row_count
    band_count, capacity = requests.shape[2:]
    slab = lax.axis_index("slab")
    subject = lax.axis_index("subj")
    last = lax.axis_size("slab") - 1
    here = slab % RING
    core = subject % 2
    chip = subject // 2
    fixed = [last, lax.axis_size("subj"), line_count, cell_count // LANES]
    place = jnp.stack([here, core, slab, fixed[0], chip, fixed[1], fixed[2], fixed[3]]).astype(I32)
    lists = requests.reshape(band_count, capacity)
    lines = template.reshape(line_count, cell_count)
    parts = cell_count // LANES
    packed = f32s(capacity * parts, LANES)

    message = jax.ShapeDtypeStruct((2, capacity), I32)
    self_lists, *messages = call(
        request_kernel, (jax.ShapeDtypeStruct((3, capacity), I32),) + (message,) * 3, [SMEM, VMEM], (VMEM,) * 4,
    )(place, lists)
    plane = call(
        spread_plane_kernel, f32s(row_count * parts, LANES), [SMEM, VMEM], VMEM,
    )(place, lines)
    spread = call(spread_kernel, f32s(line_count * parts, LANES), [VMEM], VMEM)(lines)
    from_low = along_z(plane, 1)
    from_high = along_z(plane, -1)
    asked = [self_lists] + ring_of(along_x, messages, -1)

    own = call(
        own_lines_kernel, (packed,) * 3, [SMEM] * 3 + [VMEM], (VMEM,) * 3,
    )(*asked[1:], spread)
    got_own = ring_of(along_x, own, 1)
    from_low, from_high, _ = lax.optimization_barrier((from_low, from_high, (got_own[0], got_own[2])))
    from_low_b, from_high_b = other_core(from_low), other_core(from_high)
    slabs = (from_low, from_low_b, from_high, from_high_b)
    held_slabs = [pltpu.VMEM((2 * line_count * parts, LANES), F32)]
    cross = call(
        cross_lines_kernel, (packed,) * 3, [SMEM] * 3 + [VMEM] * 4, (VMEM,) * 3, held_slabs,
    )(*asked[1:], *slabs)
    got_cross = ring_of(along_x, cross, 1)
    self_low, self_high, self_own = call(
        self_lines_kernel, (packed,) * 3, [SMEM] + [VMEM] * 5, (VMEM,) * 3, held_slabs,
    )(self_lists, spread, *slabs)

    slot_ids = corners.reshape(4, line_count)
    offset = slot_ids // capacity - REACH
    source = here + offset
    outside = (source < 0) | (source >= RING)
    behind = (here - source) % RING
    held_at = jnp.where(
        behind == 0,
        jnp.where(offset == 0, 8, jnp.where(offset < 0, 3, 4)),
        behind + jnp.where(outside, -1, 4),
    )
    slot_ids = held_at * capacity + slot_ids % capacity
    flat_ids = slot_ids.reshape(1, 4 * line_count)
    blocks = got_cross + [self_low, self_high] + got_own + [self_own]
    here_part, ahead_part = call(
        weight_kernel, (f32s(4, line_count, cell_count),) * 2, [VMEM], (VMEM,) * 2,
    )(fractions.reshape(3, line_count, cell_count))
    half = f32s(row_count, cell_count)
    push_part = jax.ShapeDtypeStruct((4 * line_count, cell_count), BF16)
    warped_0, warped_1, push_high, push_low = call(
        warp_kernel,
        (half,) * 2 + (push_part,) * 2,
        [SMEM] + [VMEM] * 12,
        (VMEM,) * 4,
        [
            pltpu.VMEM((band_count * capacity * parts, LANES), F32),
            pltpu.VMEM((4 * WARP_ROWS * parts, LANES), F32),
            pltpu.VMEM((4 * WARP_ROWS * parts, LANES), F32),
        ],
    )(slot_ids * parts, here_part, ahead_part, images.reshape(line_count, cell_count), *blocks)

    block = f32s(capacity, cell_count)
    pool_cross = call(
        functools.partial(slot_sum_kernel, 0), (block,) * 3, [VMEM] * 3, (VMEM,) * 3,
    )(flat_ids, push_high, push_low)
    pool_low, pool_high, *pool_own = call(
        functools.partial(slot_sum_kernel, 3), (block,) * 6, [VMEM] * 3, (VMEM,) * 6,
    )(flat_ids, push_high, push_low)
    back_cross = ring_of(along_x, pool_cross, -1)
    image_lines = images.reshape(line_count, cell_count)
    force = f32s(3, plane_count, row_count, cell_count)
    part_force = call(
        plane_force_kernel, force, [VMEM] * 3, ANY,
        [pltpu.VMEM((2, plane_count, row_count, cell_count), F32), pltpu.SemaphoreType.DMA],
    )(warped_0, warped_1, image_lines)
    back_cross, pool_own, part_force = lax.optimization_barrier((back_cross, pool_own, part_force))
    back_own = ring_of(along_x, pool_own, -1)

    per_piece = row_count // (2 * RING)
    wide = per_piece + 2 * HALO
    at = jnp.arange(2 * RING * 2 * wide, dtype=I32)
    piece = at // (2 * wide)
    part = jnp.where(piece < RING, core, 1 - core)
    index = part * RING + (chip + piece) % RING
    row = index * per_piece - HALO + at % wide
    target = jnp.where((row >= 0) & (row < row_count), at // wide % 2 * row_count + row, -(2**20))
    target = target.reshape(-1, 1)
    core_part = f32s(RING * 2 * wide, cell_count)
    core_rows = core_part.shape[0]
    all_rows = 2 * core_rows
    hot_own, hot_low, hot_high = call(
        line_hot_kernel,
        (jax.ShapeDtypeStruct((all_rows, 8 * capacity), BF16),) + (jax.ShapeDtypeStruct((all_rows, 10 * capacity), BF16),) * 2,
        [SMEM] + [VMEM] * 5, (VMEM,) * 3,
    )(place, *asked, target)
    keep_low, keep_high, send = call(
        cross_back_kernel, (core_part,) * 2 + (f32s(2 * core_rows, cell_count),),
        [VMEM] * 7, (VMEM,) * 3,
    )(hot_low, hot_high, pool_low, pool_high, *back_cross)
    received = other_core(send)
    sum_low = keep_low + received[:core_rows]
    sum_high = keep_high + received[core_rows:]
    in_from_high = along_z(sum_low, -1)
    in_from_low = along_z(sum_high, 1)
    back_own, sum_low, sum_high = lax.optimization_barrier((back_own, sum_low, sum_high))
    size = 2 * wide
    keep_own, *send_own = call(
        own_back_kernel, (core_part, f32s(core_rows - size, cell_count), f32s(size, cell_count)),
        [VMEM] * 5, (VMEM,) * 3,
    )(hot_own, pool_own[3], *back_own)
    got_parts = [other_core(part) for part in send_own]
    pieces = [
        keep_own[at * size:(at + 1) * size]
        + (got_parts[0][at * size:(at + 1) * size] if at < RING - 1 else got_parts[1])
        + in_from_high[at * size:(at + 1) * size]
        + in_from_low[at * size:(at + 1) * size]
        for at in range(RING)
    ]
    got_pieces = ring_of(along_y, pieces[1:], 1)
    piece_sum = pieces[0] + got_pieces[0] + got_pieces[1] + got_pieces[2]
    edge_0, edge_1, _ = lax.optimization_barrier((warped_0, warped_1, piece_sum))
    edge_before, edge_after = along_slab(edge_1, 1), along_slab(edge_0, -1)
    before, after = along_slab(piece_sum, 1), along_slab(piece_sum, -1)
    new_piece = call(
        smooth_kernel, f32s(2 * per_piece, cell_count), [SMEM] + [VMEM] * 4, VMEM,
        [pltpu.VMEM((3 * size, cell_count), F32)],
    )(place, before, piece_sum, after, lines)

    mine = [new_piece] + ring_of(along_y, [new_piece] * 3, 1)
    theirs = [other_core(value) for value in mine]
    new_template, image_force = call(
        finish_kernel, (f32s(line_count, cell_count), force), [SMEM] + [VMEM] * 5 + [ANY] * 9, (ANY, ANY),
        [pltpu.VMEM((plane_count, row_count, cell_count), F32), pltpu.SemaphoreType.DMA((4 * RING + 2,))],
        {14: 1},
    )(place, edge_before, warped_0, warped_1, edge_after, image_lines, *mine, *theirs, part_force)
    return new_template.reshape(template.shape), image_force[None]


def solution(mesh):
    return jax.shard_map(
        on_device,
        mesh=mesh,
        in_specs=(
            P("slab", None, None),
            P("subj", "slab", None, None),
            P("subj", None, "slab", None, None),
            P("subj", "slab", None, None),
            P("subj", None, "slab", None),
        ),
        out_specs=(P("slab", None, None), P("subj", None, "slab", None, None)),
        check_vma=False,
    )
```

```python
import functools

import jax
import jax.numpy as jnp
from jax import lax
from jax.experimental import pallas as pl
from jax.experimental.pallas import tpu as pltpu
from jax.sharding import PartitionSpec as P

SMOOTH = 2
REACH = 4
RING = 4
diffusion = 0.15
HALO = SMOOTH
LANES = 128
WARP_ROWS = 32

F32 = jnp.float32
BF16 = jnp.bfloat16
I32 = jnp.int32
VMEM = pl.BlockSpec(memory_space=pltpu.VMEM)
SMEM = pl.BlockSpec(memory_space=pltpu.SMEM)
ANY = pl.BlockSpec(memory_space=pl.ANY)
LIMIT = 8 * 2**20


def call(body, outs, in_specs, out_specs, scratch=(), aliases={}):
    return pl.pallas_call(
        body,
        out_shape=outs,
        in_specs=in_specs,
        out_specs=out_specs,
        scratch_shapes=list(scratch),
        input_output_aliases=aliases,
        compiler_params=pltpu.CompilerParams(vmem_limit_bytes=LIMIT),
    )


def f32s(*shape):
    return jax.ShapeDtypeStruct(shape, F32)


def along_x(value, step):
    count = lax.axis_size("slab")
    route = [(i, i // RING * RING + (i + step) % RING) for i in range(count)]
    return lax.ppermute(value, "slab", route)


def along_slab(value, step):
    count = lax.axis_size("slab")
    return lax.ppermute(value, "slab", [(i, (i + step) % count) for i in range(count)])


def along_z(value, step):
    return along_slab(value, RING * step)


def ring_of(move, values, sign):
    moved = {step: move(values[step - 1], sign * step) for step in (2, 1, 3)}
    return [moved[step] for step in (1, 2, 3)]


def other_core(value):
    count = lax.axis_size("subj")
    return lax.ppermute(value, "subj", [(i, i ^ 1) for i in range(count)])


def along_y(value, step):
    count = lax.axis_size("subj")
    return lax.ppermute(value, "subj", [(i, (i + 2 * step) % count) for i in range(count)])


def spread_rows(source_ref, start, count, out_ref):
    parts = source_ref.shape[1] // LANES

    def group(block, carry):
        first = pl.multiple_of(block * 8, 8)
        for part in range(parts):
            out_ref[pl.ds(first * parts + part, 8, stride=parts), :] = source_ref[
                pl.ds(pl.multiple_of(start + first, 8), 8), part * LANES:(part + 1) * LANES
            ]
        return carry

    lax.fori_loop(0, count // 8, group, 0, unroll=4)


def spread_plane_kernel(place_ref, source_ref, out_ref):
    rows = source_ref.shape[0] // 2
    spread_rows(source_ref, place_ref[1] * rows, rows, out_ref)


def spread_kernel(source_ref, out_ref):
    spread_rows(source_ref, 0, source_ref.shape[0], out_ref)


def request_kernel(place_ref, lists_ref, self_ref, out_1, out_2, out_3):
    here = place_ref[0]
    line_count = place_ref[6]
    parts = place_ref[7]
    flip = place_ref[1] * (line_count // 2) * parts

    def across(row, above):
        return ((lists_ref[pl.ds(row, 1), :] * parts) ^ flip) + above * line_count * parts

    self_ref[0:1, :] = lists_ref[REACH:REACH + 1, :] * parts
    self_ref[1:2, :] = across(0, 0)
    self_ref[2:3, :] = across(2 * REACH, 1)
    for step, out in ((1, out_1), (2, out_2), (3, out_3)):
        server = lax.rem(here + RING - step, RING)
        above = (here > server).astype(I32)
        out[0:1, :] = lists_ref[pl.ds(server - here + REACH, 1), :] * parts
        out[1:2, :] = across(server - here + 2 * REACH * above, above)


def fill(held, parts):
    size = parts[0].shape[0]
    unit = 64
    for at, part in enumerate(parts):
        def group(block, carry):
            first = pl.multiple_of(block * unit, unit)
            held[pl.ds(at * size + first, unit), :] = part[pl.ds(first, unit), :]
            return carry

        lax.fori_loop(0, size // unit, group, 0, unroll=4)


def copy_lines(list_ref, list_row, held, out_ref):
    count = list_ref.shape[1]
    parts = out_ref.shape[0] // count
    unit = 16

    def group(block, carry):
        found = [
            held[pl.ds(pl.multiple_of(list_ref[list_row, block * unit + at], parts), parts), :] for at in range(unit)
        ]
        for at in range(unit):
            place = pl.multiple_of((block * unit + at) * parts, parts)
            out_ref[pl.ds(place, parts), :] = found[at]
        return carry

    lax.fori_loop(0, count // unit, group, 0, unroll=2)


def near_lines_kernel(lists_1, lists_3, held, out_1, out_3):
    for lists, out in ((lists_1, out_1), (lists_3, out_3)):
        copy_lines(lists, 0, held, out)


def far_lines_kernel(lists, held, out):
    copy_lines(lists, 0, held, out)


def cross_lines_kernel(lists_1, lists_2, lists_3, low_a, low_b, high_a, high_b, out_1, out_2, out_3, held):
    fill(held, (low_a, low_b, high_a, high_b))
    for lists, out in ((lists_1, out_1), (lists_2, out_2), (lists_3, out_3)):
        copy_lines(lists, 1, held, out)


def self_lines_kernel(lists, own, low_a, low_b, high_a, high_b, out_low, out_high, out_own, held):
    fill(held, (low_a, low_b, high_a, high_b))
    copy_lines(lists, 0, own, out_own)
    copy_lines(lists, 1, held, out_low)
    copy_lines(lists, 2, held, out_high)


def split_parts(value):
    high = value.astype(BF16)
    low = (value - high.astype(F32)).astype(BF16)
    return high, low


def shift_down(value):
    width = value.shape[1]
    lane = lax.broadcasted_iota(I32, value.shape, 1)
    return jnp.where(lane == width - 1, 0.0, pltpu.roll(value, width - 1, 1))


def shift_up(value):
    lane = lax.broadcasted_iota(I32, value.shape, 1)
    return jnp.where(lane == 0, 0.0, pltpu.roll(value, 1, 1))


def corner_parts(scale, depth_part, row_part):
    above, below = scale * depth_part, scale * (1.0 - depth_part)
    rest = 1.0 - row_part
    return below * rest, below * row_part, above * rest, above * row_part


def weight_kernel(fraction_ref, here_ref, ahead_ref):
    line_count, width = fraction_ref.shape[1:]
    rows = 16
    lane = lax.broadcasted_iota(I32, (rows, width), 1)

    def step(block, carry):
        first = pl.multiple_of(block * rows, rows)
        depth_part, row_part, across = [fraction_ref[at, pl.ds(first, rows), :].astype(F32) for at in range(3)]
        here = corner_parts(1.0 - across, depth_part, row_part)
        ahead = corner_parts(
            jnp.where(lane == 0, 0.0, pltpu.roll(across, 1, 1)),
            pltpu.roll(depth_part, 1, 1), pltpu.roll(row_part, 1, 1),
        )
        for corner in range(4):
            here_ref[corner, pl.ds(first, rows), :] = here[corner]
            ahead_ref[corner, pl.ds(first, rows), :] = ahead[corner]
        return carry

    lax.fori_loop(0, line_count // rows, step, 0)


def warp_kernel(*refs):
    slot_ref, here_ref, ahead_ref, image_ref = refs[:4]
    blocks = refs[4:13]
    warped_refs, push_high, push_low = refs[13:15], refs[15], refs[16]
    held, stage_0, stage_1 = refs[17:]
    line_count, width = image_ref.shape
    parts = width // LANES
    rows_plane = line_count // 2
    rows = WARP_ROWS
    fill(held, blocks)

    def gather(block, stage, corner, low, high):
        first = block * rows
        found = []
        for row in range(low, high):
            line = slot_ref[corner, first + row]
            found.append(held[pl.ds(pl.multiple_of(line, parts), parts), :])
        for row in range(low, high):
            at = (corner * rows + row) * parts
            stage[at:at + parts, :] = found[row - low]

    lane = lax.broadcasted_iota(I32, (rows, width), 1)

    def combine(plane, block, stage, following, stage_after):
        first = pl.multiple_of(block * rows, rows)
        near, far = None, None
        for corner in range(4):
            lines = jnp.concatenate(
                [stage[pl.ds(corner * rows * parts + part, rows, stride=parts), :] for part in range(parts)],
                axis=1,
            )
            near_term = here_ref[corner, pl.ds(first, rows), :] * lines
            far_term = ahead_ref[corner, pl.ds(first, rows), :] * lines
            gather(following, stage_after, corner, 0, rows // 2)
            near = near_term if near is None else near + near_term
            far = far_term if far is None else far + far_term
        warped = near + jnp.where(lane == width - 1, 0.0, pltpu.roll(far, width - 1, 1))
        warped_refs[plane][pl.ds(pl.multiple_of(first - plane * rows_plane, rows), rows), :] = warped
        mismatch = warped - image_ref[pl.ds(first, rows), :]
        behind = pltpu.roll(mismatch, 1, 1)
        for corner in range(4):
            here, ahead = here_ref[corner, pl.ds(first, rows), :], ahead_ref[corner, pl.ds(first, rows), :]
            high, low = split_parts(here * mismatch + ahead * behind)
            gather(following, stage_after, corner, rows // 2, rows)
            at = pl.multiple_of(corner * line_count + first, rows)
            push_high[pl.ds(at, rows), :] = high
            push_low[pl.ds(at, rows), :] = low

    blocks_plane = rows_plane // rows
    last = 2 * blocks_plane - 1
    for corner in range(4):
        gather(0, stage_0, corner, 0, rows)
    for plane in range(2):
        def step(pair, carry):
            block = plane * blocks_plane + 2 * pair
            combine(plane, block, stage_0, block + 1, stage_1)
            combine(plane, block + 1, stage_1, jnp.minimum(block + 2, last), stage_0)
            return carry

        lax.fori_loop(0, blocks_plane // 2, step, 0)


def slot_sum_kernel(first, ids_ref, push_high, push_low, *outs):
    capacity = outs[0].shape[0]
    slot = lax.broadcasted_iota(I32, (capacity, push_high.shape[0]), 0)
    for start in range(0, len(outs), 3):
        chosen = outs[start:start + 3]
        hot = jnp.concatenate(
            [
                jnp.where(ids_ref[...] == slot + (first + start + at) * capacity, 1.0, 0.0).astype(BF16)
                for at in range(len(chosen))
            ],
            axis=0,
        )
        summed = jnp.dot(hot, push_high[...], preferred_element_type=F32)
        summed = summed + jnp.dot(hot, push_low[...], preferred_element_type=F32)
        for at, out in enumerate(chosen):
            out[...] = summed[at * capacity:(at + 1) * capacity]


def line_hot_kernel(place_ref, lists_0, lists_1, lists_2, lists_3, rows_ref, own_ref, low_ref, high_ref):
    capacity = lists_0.shape[1]
    line_count, parts = place_ref[6], place_ref[7]
    flip = place_ref[1] * (line_count // 2) * parts
    rows = rows_ref[...] * parts

    def hot(ids):
        return jnp.where(rows == ids, 1.0, 0.0).astype(BF16)

    own_lists = (lists_0[0:1, :], lists_1[0:1, :], lists_2[0:1, :], lists_3[0:1, :])
    cross_lists = (lists_0[1:2, :], lists_0[2:3, :], lists_1[1:2, :], lists_2[1:2, :], lists_3[1:2, :])
    for at, ids in enumerate(own_lists + own_lists):
        own_ref[:, at * capacity:(at + 1) * capacity] = hot(ids)
    for at, ids in enumerate(cross_lists + cross_lists):
        ids = ids ^ flip
        low_ref[:, at * capacity:(at + 1) * capacity] = hot(ids)
        high_ref[:, at * capacity:(at + 1) * capacity] = hot(ids - line_count * parts)


def stacked_parts(blocks):
    return jnp.concatenate(split_parts(jnp.concatenate([block[...] for block in blocks], axis=0)), axis=0)


def own_back_kernel(hot_ref, in_0, in_1, in_2, in_3, keep, send_0, send_1):
    summed = jnp.dot(hot_ref[...], stacked_parts((in_0, in_1, in_2, in_3)), preferred_element_type=F32)
    count, first = keep.shape[0], send_0.shape[0]
    keep[...] = summed[:count]
    send_0[...] = summed[count:count + first]
    send_1[...] = summed[count + first:]


def cross_send_kernel(hot_low, hot_high, in_low, in_high, in_1, in_2, in_3, send, values):
    stacked = stacked_parts((in_low, in_high, in_1, in_2, in_3))
    count = send.shape[0] // 2
    for at, hot in enumerate((hot_low, hot_high)):
        send[at * count:(at + 1) * count] = jnp.dot(hot[count:], stacked, preferred_element_type=F32)
    values[...] = stacked


def cross_keep_kernel(hot_low, hot_high, values, keep_low, keep_high):
    count = keep_low.shape[0]
    keep_low[...] = jnp.dot(hot_low[:count], values[...], preferred_element_type=F32)
    keep_high[...] = jnp.dot(hot_high[:count], values[...], preferred_element_type=F32)


def smooth_kernel(place_ref, before, piece, after, template_ref, out, field):
    device, last, core, chip = place_ref[2], place_ref[3], place_ref[1], place_ref[4]
    size = piece.shape[0]
    rows = size // 2
    total = 3 * size
    zero = jnp.zeros(piece.shape, F32)
    field[0:size, :] = jnp.where(device > 0, before[...], zero)
    field[size:2 * size, :] = piece[...]
    field[2 * size:3 * size, :] = jnp.where(device < last, after[...], zero)
    width = piece.shape[1]
    at = lax.broadcasted_iota(I32, (total, width), 0)
    row = lax.rem(at, rows)
    per_piece = rows - 2 * HALO
    index = core * RING + chip
    row = row + index * per_piece - HALO
    inside = (row >= 0) & (row < 2 * RING * per_piece)
    inside = inside & ((at >= size) | (device > 0)) & ((at < 2 * size) | (device < last))
    current = field[...]
    for repeat in range(SMOOTH):
        beside = pltpu.roll(current, rows, 0) + pltpu.roll(current, total - rows, 0)
        beside = beside + pltpu.roll(current, 1, 0) + pltpu.roll(current, total - 1, 0)
        beside = beside + shift_up(current) + shift_down(current)
        current = current + diffusion * (beside - 6.0 * current)
        if repeat < SMOOTH - 1:
            current = jnp.where(inside, current, 0.0)
    field[...] = current
    subjects = place_ref[5].astype(F32)
    plane_rows = template_ref.shape[0] // 2
    for plane in range(2):
        start = pl.multiple_of(plane * plane_rows + index * per_piece, per_piece)
        found = field[pl.ds(size + plane * rows + HALO, per_piece), :]
        out[plane * per_piece:(plane + 1) * per_piece, :] = (
            template_ref[pl.ds(start, per_piece), :] - found / subjects
        )


def plane_force_kernel(plane_0, plane_1, image_ref, out, held, sem):
    rows_plane, width = plane_0.shape
    rows = 32
    row = lax.broadcasted_iota(I32, (rows, width), 0)
    for plane, current in enumerate((plane_0, plane_1)):
        def step(block, carry):
            first = pl.multiple_of(block * rows, rows)
            centre = current[pl.ds(first, rows), :]
            negative = image_ref[pl.ds(plane * rows_plane + first, rows), :] - centre
            above = current[pl.ds(jnp.maximum(first - 1, 0), 1), :]
            above = jnp.where(first > 0, above, 0.0)
            below = current[pl.ds(jnp.minimum(first + rows, rows_plane - 1), 1), :]
            below = jnp.where(first + rows < rows_plane, below, 0.0)
            up = jnp.where(row == 0, above, pltpu.roll(centre, 1, 0))
            down = jnp.where(row == rows - 1, below, pltpu.roll(centre, rows - 1, 0))
            held[0, plane, pl.ds(first, rows), :] = negative * (0.5 * (down - up))
            held[1, plane, pl.ds(first, rows), :] = negative * (0.5 * (shift_down(centre) - shift_up(centre)))
            return carry

        lax.fori_loop(0, rows_plane // rows, step, 0)
    copy = pltpu.make_async_copy(held, out.at[pl.ds(1, 2)], sem)
    copy.start()
    copy.wait()


def finish_kernel(place_ref, before, plane_0, plane_1, after, image_ref, *refs):
    pieces = refs[:2 * RING]
    template_out, out, held, sems = refs[2 * RING + 1:]
    device, last, core, chip = place_ref[2], place_ref[3], place_ref[1], place_ref[4]
    count = pieces[0].shape[0] // 2
    rows_plane = plane_0.shape[0]
    copies = []
    for at, piece in enumerate(pieces):
        part = core if at < RING else 1 - core
        index = part * RING + lax.rem(chip + RING - at % RING, RING)
        for plane in range(2):
            start = pl.multiple_of(plane * rows_plane + index * count, count)
            copies.append(
                pltpu.make_async_copy(
                    piece.at[pl.ds(plane * count, count)], template_out.at[pl.ds(start, count)], sems.at[2 * at + plane]
                )
            )
    for copy in copies:
        copy.start()
    rows = 32
    for plane in range(2):
        def step(block, carry):
            at = pl.ds(pl.multiple_of(block * rows, rows), rows)
            image = image_ref[pl.ds(pl.multiple_of(plane * rows_plane + block * rows, rows), rows), :]
            if plane == 0:
                centre, back, ahead = plane_0[at, :], jnp.where(device > 0, before[at, :], 0.0), plane_1[at, :]
            else:
                centre, back, ahead = plane_1[at, :], plane_0[at, :], jnp.where(device < last, after[at, :], 0.0)
            held[plane, at, :] = (image - centre) * (0.5 * (ahead - back))
            return carry

        lax.fori_loop(0, rows_plane // rows, step, 0)
        copy = pltpu.make_async_copy(held.at[plane], out.at[0, plane], sems.at[4 * RING + plane])
        copy.start()
        copies.append(copy)
    for copy in copies:
        copy.wait()


def on_device(template, images, fractions, requests, corners):
    _, plane_count, row_count, cell_count = images.shape
    line_count = plane_count * row_count
    band_count, capacity = requests.shape[2:]
    slab = lax.axis_index("slab")
    subject = lax.axis_index("subj")
    last = lax.axis_size("slab") - 1
    here = slab % RING
    core = subject % 2
    chip = subject // 2
    fixed = [last, lax.axis_size("subj"), line_count, cell_count // LANES]
    place = jnp.stack([here, core, slab, fixed[0], chip, fixed[1], fixed[2], fixed[3]]).astype(I32)
    lists = requests.reshape(band_count, capacity)
    lines = template.reshape(line_count, cell_count)
    parts = cell_count // LANES
    packed = f32s(capacity * parts, LANES)

    message = jax.ShapeDtypeStruct((2, capacity), I32)
    self_lists, *messages = call(
        request_kernel, (jax.ShapeDtypeStruct((3, capacity), I32),) + (message,) * 3, [SMEM, VMEM], (VMEM,) * 4,
    )(place, lists)
    plane = call(
        spread_plane_kernel, f32s(row_count * parts, LANES), [SMEM, VMEM], VMEM,
    )(place, lines)
    spread = call(spread_kernel, f32s(line_count * parts, LANES), [VMEM], VMEM)(lines)
    from_low = along_z(plane, 1)
    from_high = along_z(plane, -1)
    asked = [self_lists] + lax.optimization_barrier(ring_of(along_x, messages, -1))

    own_1, own_3 = call(
        near_lines_kernel, (packed,) * 2, [SMEM] * 2 + [VMEM], (VMEM,) * 2,
    )(asked[1], asked[3], spread)
    got_1, got_3 = along_x(own_1, 1), along_x(own_3, 3)
    from_low, from_high, _ = lax.optimization_barrier((from_low, from_high, (got_1, got_3)))
    far_list, _ = lax.optimization_barrier((asked[2], got_3))
    own_2 = call(far_lines_kernel, packed, [SMEM, VMEM], VMEM)(far_list, spread)
    got_own = [got_1, along_x(own_2, 2), got_3]
    from_low_b, from_high_b = other_core(from_low), other_core(from_high)
    slabs = (from_low, from_low_b, from_high, from_high_b)
    held_slabs = [pltpu.VMEM((2 * line_count * parts, LANES), F32)]
    cross = call(
        cross_lines_kernel, (packed,) * 3, [SMEM] * 3 + [VMEM] * 4, (VMEM,) * 3, held_slabs,
    )(*asked[1:], *slabs)
    got_cross = ring_of(along_x, cross, 1)
    self_low, self_high, self_own = call(
        self_lines_kernel, (packed,) * 3, [SMEM] + [VMEM] * 5, (VMEM,) * 3, held_slabs,
    )(self_lists, spread, *slabs)

    slot_ids = corners.reshape(4, line_count)
    offset = slot_ids // capacity - REACH
    source = here + offset
    outside = (source < 0) | (source >= RING)
    behind = (here - source) % RING
    held_at = jnp.where(
        behind == 0,
        jnp.where(offset == 0, 8, jnp.where(offset < 0, 3, 4)),
        behind + jnp.where(outside, -1, 4),
    )
    slot_ids = held_at * capacity + slot_ids % capacity
    flat_ids = slot_ids.reshape(1, 4 * line_count)
    blocks = got_cross + [self_low, self_high] + got_own + [self_own]
    here_part, ahead_part = call(
        weight_kernel, (f32s(4, line_count, cell_count),) * 2, [VMEM], (VMEM,) * 2,
    )(fractions.reshape(3, line_count, cell_count))
    half = f32s(row_count, cell_count)
    push_part = jax.ShapeDtypeStruct((4 * line_count, cell_count), BF16)
    warped_0, warped_1, push_high, push_low = call(
        warp_kernel,
        (half,) * 2 + (push_part,) * 2,
        [SMEM] + [VMEM] * 12,
        (VMEM,) * 4,
        [
            pltpu.VMEM((band_count * capacity * parts, LANES), F32),
            pltpu.VMEM((4 * WARP_ROWS * parts, LANES), F32),
            pltpu.VMEM((4 * WARP_ROWS * parts, LANES), F32),
        ],
    )(slot_ids * parts, here_part, ahead_part, images.reshape(line_count, cell_count), *blocks)

    block = f32s(capacity, cell_count)
    pool_cross = call(
        functools.partial(slot_sum_kernel, 0), (block,) * 3, [VMEM] * 3, (VMEM,) * 3,
    )(flat_ids, push_high, push_low)
    pool_low, pool_high, *pool_own = call(
        functools.partial(slot_sum_kernel, 3), (block,) * 6, [VMEM] * 3, (VMEM,) * 6,
    )(flat_ids, push_high, push_low)
    back_cross = ring_of(along_x, pool_cross, -1)
    image_lines = images.reshape(line_count, cell_count)
    force = f32s(3, plane_count, row_count, cell_count)
    part_force = call(
        plane_force_kernel, force, [VMEM] * 3, ANY,
        [pltpu.VMEM((2, plane_count, row_count, cell_count), F32), pltpu.SemaphoreType.DMA],
    )(warped_0, warped_1, image_lines)
    back_cross, pool_own, part_force = lax.optimization_barrier((back_cross, pool_own, part_force))
    back_own = ring_of(along_x, pool_own, -1)

    per_piece = row_count // (2 * RING)
    wide = per_piece + 2 * HALO
    at = jnp.arange(2 * RING * 2 * wide, dtype=I32)
    piece = at // (2 * wide)
    part = jnp.where(piece < RING, core, 1 - core)
    index = part * RING + (chip + piece) % RING
    row = index * per_piece - HALO + at % wide
    target = jnp.where((row >= 0) & (row < row_count), at // wide % 2 * row_count + row, -(2**20))
    target = target.reshape(-1, 1)
    core_part = f32s(RING * 2 * wide, cell_count)
    core_rows = core_part.shape[0]
    all_rows = 2 * core_rows
    hot_own, hot_low, hot_high = call(
        line_hot_kernel,
        (jax.ShapeDtypeStruct((all_rows, 8 * capacity), BF16),) + (jax.ShapeDtypeStruct((all_rows, 10 * capacity), BF16),) * 2,
        [SMEM] + [VMEM] * 5, (VMEM,) * 3,
    )(place, *asked, target)
    send, stacked = call(
        cross_send_kernel,
        (f32s(2 * core_rows, cell_count), jax.ShapeDtypeStruct((10 * capacity, cell_count), BF16)),
        [VMEM] * 7, (VMEM,) * 2,
    )(hot_low, hot_high, pool_low, pool_high, *back_cross)
    keep_low, keep_high = call(
        cross_keep_kernel, (core_part,) * 2, [VMEM] * 3, (VMEM,) * 2,
    )(hot_low, hot_high, stacked)
    received = other_core(send)
    sum_low = keep_low + received[:core_rows]
    sum_high = keep_high + received[core_rows:]
    in_from_high = along_z(sum_low, -1)
    in_from_low = along_z(sum_high, 1)
    back_own, sum_low, sum_high = lax.optimization_barrier((back_own, sum_low, sum_high))
    size = 2 * wide
    keep_own, *send_own = call(
        own_back_kernel, (core_part, f32s(core_rows - size, cell_count), f32s(size, cell_count)),
        [VMEM] * 5, (VMEM,) * 3,
    )(hot_own, pool_own[3], *back_own)
    got_parts = [other_core(part) for part in send_own]
    pieces = [
        keep_own[at * size:(at + 1) * size]
        + (got_parts[0][at * size:(at + 1) * size] if at < RING - 1 else got_parts[1])
        + in_from_high[at * size:(at + 1) * size]
        + in_from_low[at * size:(at + 1) * size]
        for at in range(RING)
    ]
    got_pieces = ring_of(along_y, pieces[1:], 1)
    piece_sum = pieces[0] + got_pieces[0] + got_pieces[1] + got_pieces[2]
    edge_0, edge_1, _ = lax.optimization_barrier((warped_0, warped_1, piece_sum))
    edge_before, edge_after = along_slab(edge_1, 1), along_slab(edge_0, -1)
    before, after = along_slab(piece_sum, 1), along_slab(piece_sum, -1)
    new_piece = call(
        smooth_kernel, f32s(2 * per_piece, cell_count), [SMEM] + [VMEM] * 4, VMEM,
        [pltpu.VMEM((3 * size, cell_count), F32)],
    )(place, before, piece_sum, after, lines)

    mine = [new_piece] + ring_of(along_y, [new_piece] * 3, 1)
    theirs = [other_core(value) for value in mine]
    new_template, image_force = call(
        finish_kernel, (f32s(line_count, cell_count), force), [SMEM] + [VMEM] * 5 + [ANY] * 9, (ANY, ANY),
        [pltpu.VMEM((plane_count, row_count, cell_count), F32), pltpu.SemaphoreType.DMA((4 * RING + 2,))],
        {14: 1},
    )(place, edge_before, warped_0, warped_1, edge_after, image_lines, *mine, *theirs, part_force)
    return new_template.reshape(template.shape), image_force[None]


def solution(mesh):
    return jax.shard_map(
        on_device,
        mesh=mesh,
        in_specs=(
            P("slab", None, None),
            P("subj", "slab", None, None),
            P("subj", None, "slab", None, None),
            P("subj", "slab", None, None),
            P("subj", None, "slab", None),
        ),
        out_specs=(P("slab", None, None), P("subj", None, "slab", None, None)),
        check_vma=False,
    )
```

```python
import functools

import jax
import jax.numpy as jnp
from jax import lax
from jax.experimental import pallas as pl
from jax.experimental.pallas import tpu as pltpu
from jax.sharding import PartitionSpec as P

SMOOTH = 2
REACH = 4
RING = 4
diffusion = 0.15
HALO = SMOOTH
LANES = 128
WARP_ROWS = 32

F32 = jnp.float32
BF16 = jnp.bfloat16
I32 = jnp.int32
VMEM = pl.BlockSpec(memory_space=pltpu.VMEM)
SMEM = pl.BlockSpec(memory_space=pltpu.SMEM)
ANY = pl.BlockSpec(memory_space=pl.ANY)
LIMIT = 8 * 2**20


def call(body, outs, in_specs, out_specs, scratch=(), aliases={}):
    return pl.pallas_call(
        body,
        out_shape=outs,
        in_specs=in_specs,
        out_specs=out_specs,
        scratch_shapes=list(scratch),
        input_output_aliases=aliases,
        compiler_params=pltpu.CompilerParams(vmem_limit_bytes=LIMIT),
    )


def f32s(*shape):
    return jax.ShapeDtypeStruct(shape, F32)


def along_x(value, step):
    count = lax.axis_size("slab")
    route = [(i, i // RING * RING + (i + step) % RING) for i in range(count)]
    return lax.ppermute(value, "slab", route)


def along_slab(value, step):
    count = lax.axis_size("slab")
    return lax.ppermute(value, "slab", [(i, (i + step) % count) for i in range(count)])


def along_z(value, step):
    return along_slab(value, RING * step)


def ring_of(move, values, sign):
    moved = {step: move(values[step - 1], sign * step) for step in (2, 1, 3)}
    return [moved[step] for step in (1, 2, 3)]


def other_core(value):
    count = lax.axis_size("subj")
    return lax.ppermute(value, "subj", [(i, i ^ 1) for i in range(count)])


def along_y(value, step):
    count = lax.axis_size("subj")
    return lax.ppermute(value, "subj", [(i, (i + 2 * step) % count) for i in range(count)])


def spread_rows(source_ref, start, count, out_ref):
    parts = source_ref.shape[1] // LANES

    def group(block, carry):
        first = pl.multiple_of(block * 8, 8)
        for part in range(parts):
            out_ref[pl.ds(first * parts + part, 8, stride=parts), :] = source_ref[
                pl.ds(pl.multiple_of(start + first, 8), 8), part * LANES:(part + 1) * LANES
            ]
        return carry

    lax.fori_loop(0, count // 8, group, 0, unroll=4)


def spread_plane_kernel(place_ref, source_ref, out_ref):
    rows = source_ref.shape[0] // 2
    spread_rows(source_ref, place_ref[1] * rows, rows, out_ref)


def spread_kernel(source_ref, out_ref):
    spread_rows(source_ref, 0, source_ref.shape[0], out_ref)


def request_kernel(place_ref, lists_ref, self_ref, out_1, out_2, out_3):
    here = place_ref[0]
    line_count = place_ref[6]
    parts = place_ref[7]
    flip = place_ref[1] * (line_count // 2) * parts

    def across(row, above):
        return ((lists_ref[pl.ds(row, 1), :] * parts) ^ flip) + above * line_count * parts

    self_ref[0:1, :] = lists_ref[REACH:REACH + 1, :] * parts
    self_ref[1:2, :] = across(0, 0)
    self_ref[2:3, :] = across(2 * REACH, 1)
    for step, out in ((1, out_1), (2, out_2), (3, out_3)):
        server = lax.rem(here + RING - step, RING)
        above = (here > server).astype(I32)
        out[0:1, :] = lists_ref[pl.ds(server - here + REACH, 1), :] * parts
        out[1:2, :] = across(server - here + 2 * REACH * above, above)


def fill(held, parts):
    size = parts[0].shape[0]
    unit = 64
    for at, part in enumerate(parts):
        def group(block, carry):
            first = pl.multiple_of(block * unit, unit)
            held[pl.ds(at * size + first, unit), :] = part[pl.ds(first, unit), :]
            return carry

        lax.fori_loop(0, size // unit, group, 0, unroll=4)


def copy_lines(list_ref, list_row, held, out_ref):
    count = list_ref.shape[1]
    parts = out_ref.shape[0] // count
    unit = 16

    def group(block, carry):
        found = [
            held[pl.ds(pl.multiple_of(list_ref[list_row, block * unit + at], parts), parts), :] for at in range(unit)
        ]
        for at in range(unit):
            place = pl.multiple_of((block * unit + at) * parts, parts)
            out_ref[pl.ds(place, parts), :] = found[at]
        return carry

    lax.fori_loop(0, count // unit, group, 0, unroll=2)


def near_lines_kernel(lists_1, lists_3, held, out_1, out_3):
    for lists, out in ((lists_1, out_1), (lists_3, out_3)):
        copy_lines(lists, 0, held, out)


def far_lines_kernel(lists, held, out):
    copy_lines(lists, 0, held, out)


def cross_lines_kernel(lists_1, lists_2, lists_3, low_a, low_b, high_a, high_b, out_1, out_2, out_3, held):
    fill(held, (low_a, low_b, high_a, high_b))
    for lists, out in ((lists_1, out_1), (lists_2, out_2), (lists_3, out_3)):
        copy_lines(lists, 1, held, out)


def self_lines_kernel(lists, own, low_a, low_b, high_a, high_b, out_low, out_high, out_own, held):
    fill(held, (low_a, low_b, high_a, high_b))
    copy_lines(lists, 0, own, out_own)
    copy_lines(lists, 1, held, out_low)
    copy_lines(lists, 2, held, out_high)


def split_parts(value):
    high = value.astype(BF16)
    low = (value - high.astype(F32)).astype(BF16)
    return high, low


def shift_down(value):
    width = value.shape[1]
    lane = lax.broadcasted_iota(I32, value.shape, 1)
    return jnp.where(lane == width - 1, 0.0, pltpu.roll(value, width - 1, 1))


def shift_up(value):
    lane = lax.broadcasted_iota(I32, value.shape, 1)
    return jnp.where(lane == 0, 0.0, pltpu.roll(value, 1, 1))


def corner_parts(scale, depth_part, row_part):
    above, below = scale * depth_part, scale * (1.0 - depth_part)
    rest = 1.0 - row_part
    return below * rest, below * row_part, above * rest, above * row_part


def weight_kernel(fraction_ref, here_ref, ahead_ref):
    line_count, width = fraction_ref.shape[1:]
    rows = 16
    lane = lax.broadcasted_iota(I32, (rows, width), 1)

    def step(block, carry):
        first = pl.multiple_of(block * rows, rows)
        depth_part, row_part, across = [fraction_ref[at, pl.ds(first, rows), :].astype(F32) for at in range(3)]
        here = corner_parts(1.0 - across, depth_part, row_part)
        ahead = corner_parts(
            jnp.where(lane == 0, 0.0, pltpu.roll(across, 1, 1)),
            pltpu.roll(depth_part, 1, 1), pltpu.roll(row_part, 1, 1),
        )
        for corner in range(4):
            here_ref[corner, pl.ds(first, rows), :] = here[corner]
            ahead_ref[corner, pl.ds(first, rows), :] = ahead[corner]
        return carry

    lax.fori_loop(0, line_count // rows, step, 0)


def warp_kernel(*refs):
    slot_ref, here_ref, ahead_ref, image_ref = refs[:4]
    blocks = refs[4:13]
    warped_refs, push_high, push_low = refs[13:15], refs[15], refs[16]
    held, stage_0, stage_1 = refs[17:]
    line_count, width = image_ref.shape
    parts = width // LANES
    rows_plane = line_count // 2
    rows = WARP_ROWS
    fill(held, blocks)

    def gather(block, stage, corner, low, high):
        first = block * rows
        found = []
        for row in range(low, high):
            line = slot_ref[corner, first + row]
            found.append(held[pl.ds(pl.multiple_of(line, parts), parts), :])
        for row in range(low, high):
            at = (corner * rows + row) * parts
            stage[at:at + parts, :] = found[row - low]

    lane = lax.broadcasted_iota(I32, (rows, width), 1)

    def combine(plane, block, stage, following, stage_after):
        first = pl.multiple_of(block * rows, rows)
        near, far = None, None
        for corner in range(4):
            lines = jnp.concatenate(
                [stage[pl.ds(corner * rows * parts + part, rows, stride=parts), :] for part in range(parts)],
                axis=1,
            )
            near_term = here_ref[corner, pl.ds(first, rows), :] * lines
            far_term = ahead_ref[corner, pl.ds(first, rows), :] * lines
            gather(following, stage_after, corner, 0, rows // 2)
            near = near_term if near is None else near + near_term
            far = far_term if far is None else far + far_term
        warped = near + jnp.where(lane == width - 1, 0.0, pltpu.roll(far, width - 1, 1))
        warped_refs[plane][pl.ds(pl.multiple_of(first - plane * rows_plane, rows), rows), :] = warped
        mismatch = warped - image_ref[pl.ds(first, rows), :]
        behind = pltpu.roll(mismatch, 1, 1)
        for corner in range(4):
            here, ahead = here_ref[corner, pl.ds(first, rows), :], ahead_ref[corner, pl.ds(first, rows), :]
            high, low = split_parts(here * mismatch + ahead * behind)
            gather(following, stage_after, corner, rows // 2, rows)
            at = pl.multiple_of(corner * line_count + first, rows)
            push_high[pl.ds(at, rows), :] = high
            push_low[pl.ds(at, rows), :] = low

    blocks_plane = rows_plane // rows
    last = 2 * blocks_plane - 1
    for corner in range(4):
        gather(0, stage_0, corner, 0, rows)
    for plane in range(2):
        def step(pair, carry):
            block = plane * blocks_plane + 2 * pair
            combine(plane, block, stage_0, block + 1, stage_1)
            combine(plane, block + 1, stage_1, jnp.minimum(block + 2, last), stage_0)
            return carry

        lax.fori_loop(0, blocks_plane // 2, step, 0)


def slot_sum_kernel(first, ids_ref, push_high, push_low, *outs):
    capacity = outs[0].shape[0]
    slot = lax.broadcasted_iota(I32, (capacity, push_high.shape[0]), 0)
    for start in range(0, len(outs), 3):
        chosen = outs[start:start + 3]
        hot = jnp.concatenate(
            [
                jnp.where(ids_ref[...] == slot + (first + start + at) * capacity, 1.0, 0.0).astype(BF16)
                for at in range(len(chosen))
            ],
            axis=0,
        )
        summed = jnp.dot(hot, push_high[...], preferred_element_type=F32)
        summed = summed + jnp.dot(hot, push_low[...], preferred_element_type=F32)
        for at, out in enumerate(chosen):
            out[...] = summed[at * capacity:(at + 1) * capacity]


def line_hot_kernel(place_ref, lists_0, lists_1, lists_2, lists_3, rows_ref, own_ref, low_ref, high_ref):
    capacity = lists_0.shape[1]
    line_count, parts = place_ref[6], place_ref[7]
    flip = place_ref[1] * (line_count // 2) * parts
    rows = rows_ref[...] * parts

    def hot(ids):
        return jnp.where(rows == ids, 1.0, 0.0).astype(BF16)

    own_lists = (lists_0[0:1, :], lists_1[0:1, :], lists_2[0:1, :], lists_3[0:1, :])
    cross_lists = (lists_0[1:2, :], lists_0[2:3, :], lists_1[1:2, :], lists_2[1:2, :], lists_3[1:2, :])
    for at, ids in enumerate(own_lists + own_lists):
        own_ref[:, at * capacity:(at + 1) * capacity] = hot(ids)
    for at, ids in enumerate(cross_lists + cross_lists):
        ids = ids ^ flip
        low_ref[:, at * capacity:(at + 1) * capacity] = hot(ids)
        high_ref[:, at * capacity:(at + 1) * capacity] = hot(ids - line_count * parts)


def stacked_parts(blocks):
    return jnp.concatenate(split_parts(jnp.concatenate([block[...] for block in blocks], axis=0)), axis=0)


def own_back_kernel(hot_ref, in_0, in_1, in_2, in_3, keep, send_0, send_1):
    summed = jnp.dot(hot_ref[...], stacked_parts((in_0, in_1, in_2, in_3)), preferred_element_type=F32)
    count, first = keep.shape[0], send_0.shape[0]
    keep[...] = summed[:count]
    send_0[...] = summed[count:count + first]
    send_1[...] = summed[count + first:]


def cross_send_kernel(hot_low, hot_high, in_low, in_high, in_1, in_2, in_3, send, values):
    stacked = stacked_parts((in_low, in_high, in_1, in_2, in_3))
    count = send.shape[0] // 2
    for at, hot in enumerate((hot_low, hot_high)):
        send[at * count:(at + 1) * count] = jnp.dot(hot[count:], stacked, preferred_element_type=F32)
    values[...] = stacked


def cross_keep_kernel(hot_low, hot_high, values, keep_low, keep_high):
    count = keep_low.shape[0]
    keep_low[...] = jnp.dot(hot_low[:count], values[...], preferred_element_type=F32)
    keep_high[...] = jnp.dot(hot_high[:count], values[...], preferred_element_type=F32)


def smooth_kernel(place_ref, before, piece, after, template_ref, out, field):
    device, last, core, chip = place_ref[2], place_ref[3], place_ref[1], place_ref[4]
    size = piece.shape[0]
    rows = size // 2
    total = 3 * size
    zero = jnp.zeros(piece.shape, F32)
    field[0:size, :] = jnp.where(device > 0, before[...], zero)
    field[size:2 * size, :] = piece[...]
    field[2 * size:3 * size, :] = jnp.where(device < last, after[...], zero)
    width = piece.shape[1]
    at = lax.broadcasted_iota(I32, (total, width), 0)
    row = lax.rem(at, rows)
    per_piece = rows - 2 * HALO
    index = core * RING + chip
    row = row + index * per_piece - HALO
    inside = (row >= 0) & (row < 2 * RING * per_piece)
    inside = inside & ((at >= size) | (device > 0)) & ((at < 2 * size) | (device < last))
    current = field[...]
    for repeat in range(SMOOTH):
        beside = pltpu.roll(current, rows, 0) + pltpu.roll(current, total - rows, 0)
        beside = beside + pltpu.roll(current, 1, 0) + pltpu.roll(current, total - 1, 0)
        beside = beside + shift_up(current) + shift_down(current)
        current = current + diffusion * (beside - 6.0 * current)
        if repeat < SMOOTH - 1:
            current = jnp.where(inside, current, 0.0)
    field[...] = current
    subjects = place_ref[5].astype(F32)
    plane_rows = template_ref.shape[0] // 2
    for plane in range(2):
        start = pl.multiple_of(plane * plane_rows + index * per_piece, per_piece)
        found = field[pl.ds(size + plane * rows + HALO, per_piece), :]
        out[plane * per_piece:(plane + 1) * per_piece, :] = (
            template_ref[pl.ds(start, per_piece), :] - found / subjects
        )


def plane_force_kernel(plane_0, plane_1, image_ref, out, held, sem):
    rows_plane, width = plane_0.shape
    rows = 32
    row = lax.broadcasted_iota(I32, (rows, width), 0)
    for plane, current in enumerate((plane_0, plane_1)):
        def step(block, carry):
            first = pl.multiple_of(block * rows, rows)
            centre = current[pl.ds(first, rows), :]
            negative = image_ref[pl.ds(plane * rows_plane + first, rows), :] - centre
            above = current[pl.ds(jnp.maximum(first - 1, 0), 1), :]
            above = jnp.where(first > 0, above, 0.0)
            below = current[pl.ds(jnp.minimum(first + rows, rows_plane - 1), 1), :]
            below = jnp.where(first + rows < rows_plane, below, 0.0)
            up = jnp.where(row == 0, above, pltpu.roll(centre, 1, 0))
            down = jnp.where(row == rows - 1, below, pltpu.roll(centre, rows - 1, 0))
            held[0, plane, pl.ds(first, rows), :] = negative * (0.5 * (down - up))
            held[1, plane, pl.ds(first, rows), :] = negative * (0.5 * (shift_down(centre) - shift_up(centre)))
            return carry

        lax.fori_loop(0, rows_plane // rows, step, 0)
    copy = pltpu.make_async_copy(held, out.at[pl.ds(1, 2)], sem)
    copy.start()
    copy.wait()


def finish_kernel(place_ref, before, plane_0, plane_1, after, image_ref, *refs):
    pieces = refs[:2 * RING]
    template_out, out, held, sems = refs[2 * RING + 1:]
    device, last, core, chip = place_ref[2], place_ref[3], place_ref[1], place_ref[4]
    count = pieces[0].shape[0] // 2
    rows_plane = plane_0.shape[0]
    copies = []
    for at, piece in enumerate(pieces):
        part = core if at < RING else 1 - core
        index = part * RING + lax.rem(chip + RING - at % RING, RING)
        for plane in range(2):
            start = pl.multiple_of(plane * rows_plane + index * count, count)
            copies.append(
                pltpu.make_async_copy(
                    piece.at[pl.ds(plane * count, count)], template_out.at[pl.ds(start, count)], sems.at[2 * at + plane]
                )
            )
    for copy in copies:
        copy.start()
    rows = 32
    for plane in range(2):
        def step(block, carry):
            at = pl.ds(pl.multiple_of(block * rows, rows), rows)
            image = image_ref[pl.ds(pl.multiple_of(plane * rows_plane + block * rows, rows), rows), :]
            if plane == 0:
                centre, back, ahead = plane_0[at, :], jnp.where(device > 0, before[at, :], 0.0), plane_1[at, :]
            else:
                centre, back, ahead = plane_1[at, :], plane_0[at, :], jnp.where(device < last, after[at, :], 0.0)
            held[plane, at, :] = (image - centre) * (0.5 * (ahead - back))
            return carry

        lax.fori_loop(0, rows_plane // rows, step, 0)
        copy = pltpu.make_async_copy(held.at[plane], out.at[0, plane], sems.at[4 * RING + plane])
        copy.start()
        copies.append(copy)
    for copy in copies:
        copy.wait()


def on_device(template, images, fractions, requests, corners):
    _, plane_count, row_count, cell_count = images.shape
    line_count = plane_count * row_count
    band_count, capacity = requests.shape[2:]
    slab = lax.axis_index("slab")
    subject = lax.axis_index("subj")
    last = lax.axis_size("slab") - 1
    here = slab % RING
    core = subject % 2
    chip = subject // 2
    fixed = [last, lax.axis_size("subj"), line_count, cell_count // LANES]
    place = jnp.stack([here, core, slab, fixed[0], chip, fixed[1], fixed[2], fixed[3]]).astype(I32)
    lists = requests.reshape(band_count, capacity)
    lines = template.reshape(line_count, cell_count)
    parts = cell_count // LANES
    packed = f32s(capacity * parts, LANES)

    message = jax.ShapeDtypeStruct((2, capacity), I32)
    self_lists, *messages = call(
        request_kernel, (jax.ShapeDtypeStruct((3, capacity), I32),) + (message,) * 3, [SMEM, VMEM], (VMEM,) * 4,
    )(place, lists)
    plane = call(
        spread_plane_kernel, f32s(row_count * parts, LANES), [SMEM, VMEM], VMEM,
    )(place, lines)
    spread = call(spread_kernel, f32s(line_count * parts, LANES), [VMEM], VMEM)(lines)
    from_low = along_z(plane, 1)
    from_high = along_z(plane, -1)
    asked = [self_lists] + lax.optimization_barrier(ring_of(along_x, messages, -1))

    own_1, own_3 = call(
        near_lines_kernel, (packed,) * 2, [SMEM] * 2 + [VMEM], (VMEM,) * 2,
    )(asked[1], asked[3], spread)
    got_1, got_3 = along_x(own_1, 1), along_x(own_3, 3)
    own_2 = call(far_lines_kernel, packed, [SMEM, VMEM], VMEM)(asked[2], spread)
    from_low, from_high, own_2, _ = lax.optimization_barrier((from_low, from_high, own_2, (got_1, got_3)))
    got_own = [got_1, along_x(own_2, 2), got_3]
    from_low_b, from_high_b = other_core(from_low), other_core(from_high)
    slabs = (from_low, from_low_b, from_high, from_high_b)
    held_slabs = [pltpu.VMEM((2 * line_count * parts, LANES), F32)]
    cross = call(
        cross_lines_kernel, (packed,) * 3, [SMEM] * 3 + [VMEM] * 4, (VMEM,) * 3, held_slabs,
    )(*asked[1:], *slabs)
    got_cross = ring_of(along_x, cross, 1)
    self_low, self_high, self_own = call(
        self_lines_kernel, (packed,) * 3, [SMEM] + [VMEM] * 5, (VMEM,) * 3, held_slabs,
    )(self_lists, spread, *slabs)

    slot_ids = corners.reshape(4, line_count)
    offset = slot_ids // capacity - REACH
    source = here + offset
    outside = (source < 0) | (source >= RING)
    behind = (here - source) % RING
    held_at = jnp.where(
        behind == 0,
        jnp.where(offset == 0, 8, jnp.where(offset < 0, 3, 4)),
        behind + jnp.where(outside, -1, 4),
    )
    slot_ids = held_at * capacity + slot_ids % capacity
    flat_ids = slot_ids.reshape(1, 4 * line_count)
    blocks = got_cross + [self_low, self_high] + got_own + [self_own]
    here_part, ahead_part = call(
        weight_kernel, (f32s(4, line_count, cell_count),) * 2, [VMEM], (VMEM,) * 2,
    )(fractions.reshape(3, line_count, cell_count))
    half = f32s(row_count, cell_count)
    push_part = jax.ShapeDtypeStruct((4 * line_count, cell_count), BF16)
    warped_0, warped_1, push_high, push_low = call(
        warp_kernel,
        (half,) * 2 + (push_part,) * 2,
        [SMEM] + [VMEM] * 12,
        (VMEM,) * 4,
        [
            pltpu.VMEM((band_count * capacity * parts, LANES), F32),
            pltpu.VMEM((4 * WARP_ROWS * parts, LANES), F32),
            pltpu.VMEM((4 * WARP_ROWS * parts, LANES), F32),
        ],
    )(slot_ids * parts, here_part, ahead_part, images.reshape(line_count, cell_count), *blocks)

    block = f32s(capacity, cell_count)
    pool_cross = call(
        functools.partial(slot_sum_kernel, 0), (block,) * 3, [VMEM] * 3, (VMEM,) * 3,
    )(flat_ids, push_high, push_low)
    pool_low, pool_high, *pool_own = call(
        functools.partial(slot_sum_kernel, 3), (block,) * 6, [VMEM] * 3, (VMEM,) * 6,
    )(flat_ids, push_high, push_low)
    back_cross = ring_of(along_x, pool_cross, -1)
    image_lines = images.reshape(line_count, cell_count)
    force = f32s(3, plane_count, row_count, cell_count)
    part_force = call(
        plane_force_kernel, force, [VMEM] * 3, ANY,
        [pltpu.VMEM((2, plane_count, row_count, cell_count), F32), pltpu.SemaphoreType.DMA],
    )(warped_0, warped_1, image_lines)
    back_cross, pool_own, part_force = lax.optimization_barrier((back_cross, pool_own, part_force))
    back_own = ring_of(along_x, pool_own, -1)

    per_piece = row_count // (2 * RING)
    wide = per_piece + 2 * HALO
    at = jnp.arange(2 * RING * 2 * wide, dtype=I32)
    piece = at // (2 * wide)
    part = jnp.where(piece < RING, core, 1 - core)
    index = part * RING + (chip + piece) % RING
    row = index * per_piece - HALO + at % wide
    target = jnp.where((row >= 0) & (row < row_count), at // wide % 2 * row_count + row, -(2**20))
    target = target.reshape(-1, 1)
    core_part = f32s(RING * 2 * wide, cell_count)
    core_rows = core_part.shape[0]
    all_rows = 2 * core_rows
    hot_own, hot_low, hot_high = call(
        line_hot_kernel,
        (jax.ShapeDtypeStruct((all_rows, 8 * capacity), BF16),) + (jax.ShapeDtypeStruct((all_rows, 10 * capacity), BF16),) * 2,
        [SMEM] + [VMEM] * 5, (VMEM,) * 3,
    )(place, *asked, target)
    send, stacked = call(
        cross_send_kernel,
        (f32s(2 * core_rows, cell_count), jax.ShapeDtypeStruct((10 * capacity, cell_count), BF16)),
        [VMEM] * 7, (VMEM,) * 2,
    )(hot_low, hot_high, pool_low, pool_high, *back_cross)
    keep_low, keep_high = call(
        cross_keep_kernel, (core_part,) * 2, [VMEM] * 3, (VMEM,) * 2,
    )(hot_low, hot_high, stacked)
    received = other_core(send)
    sum_low = keep_low + received[:core_rows]
    sum_high = keep_high + received[core_rows:]
    in_from_high = along_z(sum_low, -1)
    in_from_low = along_z(sum_high, 1)
    back_own, sum_low, sum_high = lax.optimization_barrier((back_own, sum_low, sum_high))
    size = 2 * wide
    keep_own, *send_own = call(
        own_back_kernel, (core_part, f32s(core_rows - size, cell_count), f32s(size, cell_count)),
        [VMEM] * 5, (VMEM,) * 3,
    )(hot_own, pool_own[3], *back_own)
    got_parts = [other_core(part) for part in send_own]
    pieces = [
        keep_own[at * size:(at + 1) * size]
        + (got_parts[0][at * size:(at + 1) * size] if at < RING - 1 else got_parts[1])
        + in_from_high[at * size:(at + 1) * size]
        + in_from_low[at * size:(at + 1) * size]
        for at in range(RING)
    ]
    got_pieces = ring_of(along_y, pieces[1:], 1)
    piece_sum = pieces[0] + got_pieces[0] + got_pieces[1] + got_pieces[2]
    edge_0, edge_1, _ = lax.optimization_barrier((warped_0, warped_1, piece_sum))
    edge_before, edge_after = along_slab(edge_1, 1), along_slab(edge_0, -1)
    before, after = along_slab(piece_sum, 1), along_slab(piece_sum, -1)
    new_piece = call(
        smooth_kernel, f32s(2 * per_piece, cell_count), [SMEM] + [VMEM] * 4, VMEM,
        [pltpu.VMEM((3 * size, cell_count), F32)],
    )(place, before, piece_sum, after, lines)

    mine = [new_piece] + ring_of(along_y, [new_piece] * 3, 1)
    theirs = [other_core(value) for value in mine]
    new_template, image_force = call(
        finish_kernel, (f32s(line_count, cell_count), force), [SMEM] + [VMEM] * 5 + [ANY] * 9, (ANY, ANY),
        [pltpu.VMEM((plane_count, row_count, cell_count), F32), pltpu.SemaphoreType.DMA((4 * RING + 2,))],
        {14: 1},
    )(place, edge_before, warped_0, warped_1, edge_after, image_lines, *mine, *theirs, part_force)
    return new_template.reshape(template.shape), image_force[None]


def solution(mesh):
    return jax.shard_map(
        on_device,
        mesh=mesh,
        in_specs=(
            P("slab", None, None),
            P("subj", "slab", None, None),
            P("subj", None, "slab", None, None),
            P("subj", "slab", None, None),
            P("subj", None, "slab", None),
        ),
        out_specs=(P("slab", None, None), P("subj", None, "slab", None, None)),
        check_vma=False,
    )
```

```python
import functools

import jax
import jax.numpy as jnp
from jax import lax
from jax.experimental import pallas as pl
from jax.experimental.pallas import tpu as pltpu
from jax.sharding import PartitionSpec as P

SMOOTH = 2
REACH = 4
RING = 4
diffusion = 0.15
HALO = SMOOTH
LANES = 128
WARP_ROWS = 32

F32 = jnp.float32
BF16 = jnp.bfloat16
I32 = jnp.int32
VMEM = pl.BlockSpec(memory_space=pltpu.VMEM)
SMEM = pl.BlockSpec(memory_space=pltpu.SMEM)
ANY = pl.BlockSpec(memory_space=pl.ANY)
LIMIT = 8 * 2**20


def call(body, outs, in_specs, out_specs, scratch=(), aliases={}):
    return pl.pallas_call(
        body,
        out_shape=outs,
        in_specs=in_specs,
        out_specs=out_specs,
        scratch_shapes=list(scratch),
        input_output_aliases=aliases,
        compiler_params=pltpu.CompilerParams(vmem_limit_bytes=LIMIT),
    )


def f32s(*shape):
    return jax.ShapeDtypeStruct(shape, F32)


def along_x(value, step):
    count = lax.axis_size("slab")
    route = [(i, i // RING * RING + (i + step) % RING) for i in range(count)]
    return lax.ppermute(value, "slab", route)


def along_slab(value, step):
    count = lax.axis_size("slab")
    return lax.ppermute(value, "slab", [(i, (i + step) % count) for i in range(count)])


def along_z(value, step):
    return along_slab(value, RING * step)


def ring_of(move, values, sign):
    moved = {step: move(values[step - 1], sign * step) for step in (2, 1, 3)}
    return [moved[step] for step in (1, 2, 3)]


def other_core(value):
    count = lax.axis_size("subj")
    return lax.ppermute(value, "subj", [(i, i ^ 1) for i in range(count)])


def along_y(value, step):
    count = lax.axis_size("subj")
    return lax.ppermute(value, "subj", [(i, (i + 2 * step) % count) for i in range(count)])


def spread_rows(source_ref, start, count, out_ref):
    parts = source_ref.shape[1] // LANES

    def group(block, carry):
        first = pl.multiple_of(block * 8, 8)
        for part in range(parts):
            out_ref[pl.ds(first * parts + part, 8, stride=parts), :] = source_ref[
                pl.ds(pl.multiple_of(start + first, 8), 8), part * LANES:(part + 1) * LANES
            ]
        return carry

    lax.fori_loop(0, count // 8, group, 0, unroll=4)


def spread_plane_kernel(place_ref, source_ref, out_ref):
    rows = source_ref.shape[0] // 2
    spread_rows(source_ref, place_ref[1] * rows, rows, out_ref)


def spread_kernel(source_ref, out_ref):
    spread_rows(source_ref, 0, source_ref.shape[0], out_ref)


def request_kernel(place_ref, lists_ref, self_ref, out_1, out_2, out_3):
    here = place_ref[0]
    line_count = place_ref[6]
    parts = place_ref[7]
    flip = place_ref[1] * (line_count // 2) * parts

    def across(row, above):
        return ((lists_ref[pl.ds(row, 1), :] * parts) ^ flip) + above * line_count * parts

    self_ref[0:1, :] = lists_ref[REACH:REACH + 1, :] * parts
    self_ref[1:2, :] = across(0, 0)
    self_ref[2:3, :] = across(2 * REACH, 1)
    for step, out in ((1, out_1), (2, out_2), (3, out_3)):
        server = lax.rem(here + RING - step, RING)
        above = (here > server).astype(I32)
        out[0:1, :] = lists_ref[pl.ds(server - here + REACH, 1), :] * parts
        out[1:2, :] = across(server - here + 2 * REACH * above, above)


def fill(held, parts):
    size = parts[0].shape[0]
    unit = 64
    for at, part in enumerate(parts):
        def group(block, carry):
            first = pl.multiple_of(block * unit, unit)
            held[pl.ds(at * size + first, unit), :] = part[pl.ds(first, unit), :]
            return carry

        lax.fori_loop(0, size // unit, group, 0, unroll=4)


def copy_lines(list_ref, list_row, held, out_ref):
    count = list_ref.shape[1]
    parts = out_ref.shape[0] // count
    unit = 16

    def group(block, carry):
        found = [
            held[pl.ds(pl.multiple_of(list_ref[list_row, block * unit + at], parts), parts), :] for at in range(unit)
        ]
        for at in range(unit):
            place = pl.multiple_of((block * unit + at) * parts, parts)
            out_ref[pl.ds(place, parts), :] = found[at]
        return carry

    lax.fori_loop(0, count // unit, group, 0, unroll=2)


def near_lines_kernel(lists_1, lists_3, held, out_1, out_3):
    for lists, out in ((lists_1, out_1), (lists_3, out_3)):
        copy_lines(lists, 0, held, out)


def far_lines_kernel(lists, held, out):
    copy_lines(lists, 0, held, out)


def cross_lines_kernel(lists_1, lists_2, lists_3, low_a, low_b, high_a, high_b, out_1, out_2, out_3, held):
    fill(held, (low_a, low_b, high_a, high_b))
    for lists, out in ((lists_1, out_1), (lists_2, out_2), (lists_3, out_3)):
        copy_lines(lists, 1, held, out)


def self_lines_kernel(lists, own, low_a, low_b, high_a, high_b, out_low, out_high, out_own, held):
    fill(held, (low_a, low_b, high_a, high_b))
    copy_lines(lists, 0, own, out_own)
    copy_lines(lists, 1, held, out_low)
    copy_lines(lists, 2, held, out_high)


def split_parts(value):
    high = value.astype(BF16)
    low = (value - high.astype(F32)).astype(BF16)
    return high, low


def shift_down(value):
    width = value.shape[1]
    lane = lax.broadcasted_iota(I32, value.shape, 1)
    return jnp.where(lane == width - 1, 0.0, pltpu.roll(value, width - 1, 1))


def shift_up(value):
    lane = lax.broadcasted_iota(I32, value.shape, 1)
    return jnp.where(lane == 0, 0.0, pltpu.roll(value, 1, 1))


def corner_parts(scale, depth_part, row_part):
    above, below = scale * depth_part, scale * (1.0 - depth_part)
    rest = 1.0 - row_part
    return below * rest, below * row_part, above * rest, above * row_part


def weight_kernel(fraction_ref, here_ref, ahead_ref):
    line_count, width = fraction_ref.shape[1:]
    rows = 16
    lane = lax.broadcasted_iota(I32, (rows, width), 1)

    def step(block, carry):
        first = pl.multiple_of(block * rows, rows)
        depth_part, row_part, across = [fraction_ref[at, pl.ds(first, rows), :].astype(F32) for at in range(3)]
        here = corner_parts(1.0 - across, depth_part, row_part)
        ahead = corner_parts(
            jnp.where(lane == 0, 0.0, pltpu.roll(across, 1, 1)),
            pltpu.roll(depth_part, 1, 1), pltpu.roll(row_part, 1, 1),
        )
        for corner in range(4):
            here_ref[corner, pl.ds(first, rows), :] = here[corner]
            ahead_ref[corner, pl.ds(first, rows), :] = ahead[corner]
        return carry

    lax.fori_loop(0, line_count // rows, step, 0)


def warp_kernel(*refs):
    slot_ref, here_ref, ahead_ref, image_ref = refs[:4]
    blocks = refs[4:13]
    warped_refs, push_high, push_low = refs[13:15], refs[15], refs[16]
    held, stage_0, stage_1 = refs[17:]
    line_count, width = image_ref.shape
    parts = width // LANES
    rows_plane = line_count // 2
    rows = WARP_ROWS
    fill(held, blocks)

    def gather(block, stage, corner, low, high):
        first = block * rows
        found = []
        for row in range(low, high):
            line = slot_ref[corner, first + row]
            found.append(held[pl.ds(pl.multiple_of(line, parts), parts), :])
        for row in range(low, high):
            at = (corner * rows + row) * parts
            stage[at:at + parts, :] = found[row - low]

    lane = lax.broadcasted_iota(I32, (rows, width), 1)

    def combine(plane, block, stage, following, stage_after):
        first = pl.multiple_of(block * rows, rows)
        near, far = None, None
        for corner in range(4):
            lines = jnp.concatenate(
                [stage[pl.ds(corner * rows * parts + part, rows, stride=parts), :] for part in range(parts)],
                axis=1,
            )
            near_term = here_ref[corner, pl.ds(first, rows), :] * lines
            far_term = ahead_ref[corner, pl.ds(first, rows), :] * lines
            gather(following, stage_after, corner, 0, rows // 2)
            near = near_term if near is None else near + near_term
            far = far_term if far is None else far + far_term
        warped = near + jnp.where(lane == width - 1, 0.0, pltpu.roll(far, width - 1, 1))
        warped_refs[plane][pl.ds(pl.multiple_of(first - plane * rows_plane, rows), rows), :] = warped
        mismatch = warped - image_ref[pl.ds(first, rows), :]
        behind = pltpu.roll(mismatch, 1, 1)
        for corner in range(4):
            here, ahead = here_ref[corner, pl.ds(first, rows), :], ahead_ref[corner, pl.ds(first, rows), :]
            high, low = split_parts(here * mismatch + ahead * behind)
            gather(following, stage_after, corner, rows // 2, rows)
            at = pl.multiple_of(corner * line_count + first, rows)
            push_high[pl.ds(at, rows), :] = high
            push_low[pl.ds(at, rows), :] = low

    blocks_plane = rows_plane // rows
    last = 2 * blocks_plane - 1
    for corner in range(4):
        gather(0, stage_0, corner, 0, rows)
    for plane in range(2):
        def step(pair, carry):
            block = plane * blocks_plane + 2 * pair
            combine(plane, block, stage_0, block + 1, stage_1)
            combine(plane, block + 1, stage_1, jnp.minimum(block + 2, last), stage_0)
            return carry

        lax.fori_loop(0, blocks_plane // 2, step, 0)


def slot_sum_kernel(first, ids_ref, push_high, push_low, *outs):
    capacity = outs[0].shape[0]
    slot = lax.broadcasted_iota(I32, (capacity, push_high.shape[0]), 0)
    for start in range(0, len(outs), 3):
        chosen = outs[start:start + 3]
        hot = jnp.concatenate(
            [
                jnp.where(ids_ref[...] == slot + (first + start + at) * capacity, 1.0, 0.0).astype(BF16)
                for at in range(len(chosen))
            ],
            axis=0,
        )
        summed = jnp.dot(hot, push_high[...], preferred_element_type=F32)
        summed = summed + jnp.dot(hot, push_low[...], preferred_element_type=F32)
        for at, out in enumerate(chosen):
            out[...] = summed[at * capacity:(at + 1) * capacity]


def line_hot_kernel(place_ref, lists_0, lists_1, lists_2, lists_3, rows_ref, own_ref, low_ref, high_ref):
    capacity = lists_0.shape[1]
    line_count, parts = place_ref[6], place_ref[7]
    flip = place_ref[1] * (line_count // 2) * parts
    rows = rows_ref[...] * parts

    def hot(ids):
        return jnp.where(rows == ids, 1.0, 0.0).astype(BF16)

    own_lists = (lists_0[0:1, :], lists_1[0:1, :], lists_2[0:1, :], lists_3[0:1, :])
    cross_lists = (lists_0[1:2, :], lists_0[2:3, :], lists_1[1:2, :], lists_2[1:2, :], lists_3[1:2, :])
    for at, ids in enumerate(own_lists + own_lists):
        own_ref[:, at * capacity:(at + 1) * capacity] = hot(ids)
    for at, ids in enumerate(cross_lists + cross_lists):
        ids = ids ^ flip
        low_ref[:, at * capacity:(at + 1) * capacity] = hot(ids)
        high_ref[:, at * capacity:(at + 1) * capacity] = hot(ids - line_count * parts)


def stacked_parts(blocks):
    return jnp.concatenate(split_parts(jnp.concatenate([block[...] for block in blocks], axis=0)), axis=0)


def own_back_kernel(hot_ref, in_0, in_1, in_2, in_3, keep, send_0, send_1):
    summed = jnp.dot(hot_ref[...], stacked_parts((in_0, in_1, in_2, in_3)), preferred_element_type=F32)
    count, first = keep.shape[0], send_0.shape[0]
    keep[...] = summed[:count]
    send_0[...] = summed[count:count + first]
    send_1[...] = summed[count + first:]


def cross_send_kernel(hot_low, hot_high, in_low, in_high, in_1, in_2, in_3, send, values):
    stacked = stacked_parts((in_low, in_high, in_1, in_2, in_3))
    count = send.shape[0] // 2
    for at, hot in enumerate((hot_low, hot_high)):
        send[at * count:(at + 1) * count] = jnp.dot(hot[count:], stacked, preferred_element_type=F32)
    values[...] = stacked


def cross_keep_kernel(hot_low, hot_high, values, keep_low, keep_high):
    count = keep_low.shape[0]
    keep_low[...] = jnp.dot(hot_low[:count], values[...], preferred_element_type=F32)
    keep_high[...] = jnp.dot(hot_high[:count], values[...], preferred_element_type=F32)


def smooth_kernel(place_ref, before, piece, after, template_ref, out, field):
    device, last, core, chip = place_ref[2], place_ref[3], place_ref[1], place_ref[4]
    size = piece.shape[0]
    rows = size // 2
    total = 3 * size
    zero = jnp.zeros(piece.shape, F32)
    field[0:size, :] = jnp.where(device > 0, before[...], zero)
    field[size:2 * size, :] = piece[...]
    field[2 * size:3 * size, :] = jnp.where(device < last, after[...], zero)
    width = piece.shape[1]
    at = lax.broadcasted_iota(I32, (total, width), 0)
    row = lax.rem(at, rows)
    per_piece = rows - 2 * HALO
    index = core * RING + chip
    row = row + index * per_piece - HALO
    inside = (row >= 0) & (row < 2 * RING * per_piece)
    inside = inside & ((at >= size) | (device > 0)) & ((at < 2 * size) | (device < last))
    current = field[...]
    for repeat in range(SMOOTH):
        beside = pltpu.roll(current, rows, 0) + pltpu.roll(current, total - rows, 0)
        beside = beside + pltpu.roll(current, 1, 0) + pltpu.roll(current, total - 1, 0)
        beside = beside + shift_up(current) + shift_down(current)
        current = current + diffusion * (beside - 6.0 * current)
        if repeat < SMOOTH - 1:
            current = jnp.where(inside, current, 0.0)
    field[...] = current
    subjects = place_ref[5].astype(F32)
    plane_rows = template_ref.shape[0] // 2
    for plane in range(2):
        start = pl.multiple_of(plane * plane_rows + index * per_piece, per_piece)
        found = field[pl.ds(size + plane * rows + HALO, per_piece), :]
        out[plane * per_piece:(plane + 1) * per_piece, :] = (
            template_ref[pl.ds(start, per_piece), :] - found / subjects
        )


def plane_force_kernel(plane_0, plane_1, image_ref, out, held, sem):
    rows_plane, width = plane_0.shape
    rows = 32
    row = lax.broadcasted_iota(I32, (rows, width), 0)
    for plane, current in enumerate((plane_0, plane_1)):
        def step(block, carry):
            first = pl.multiple_of(block * rows, rows)
            centre = current[pl.ds(first, rows), :]
            negative = image_ref[pl.ds(plane * rows_plane + first, rows), :] - centre
            above = current[pl.ds(jnp.maximum(first - 1, 0), 1), :]
            above = jnp.where(first > 0, above, 0.0)
            below = current[pl.ds(jnp.minimum(first + rows, rows_plane - 1), 1), :]
            below = jnp.where(first + rows < rows_plane, below, 0.0)
            up = jnp.where(row == 0, above, pltpu.roll(centre, 1, 0))
            down = jnp.where(row == rows - 1, below, pltpu.roll(centre, rows - 1, 0))
            held[0, plane, pl.ds(first, rows), :] = negative * (0.5 * (down - up))
            held[1, plane, pl.ds(first, rows), :] = negative * (0.5 * (shift_down(centre) - shift_up(centre)))
            return carry

        lax.fori_loop(0, rows_plane // rows, step, 0)
    copy = pltpu.make_async_copy(held, out.at[pl.ds(1, 2)], sem)
    copy.start()
    copy.wait()


def finish_kernel(place_ref, before, plane_0, plane_1, after, image_ref, *refs):
    pieces = refs[:2 * RING]
    template_out, out, held, sems = refs[2 * RING + 1:]
    device, last, core, chip = place_ref[2], place_ref[3], place_ref[1], place_ref[4]
    count = pieces[0].shape[0] // 2
    rows_plane = plane_0.shape[0]
    copies = []
    for at, piece in enumerate(pieces):
        part = core if at < RING else 1 - core
        index = part * RING + lax.rem(chip + RING - at % RING, RING)
        for plane in range(2):
            start = pl.multiple_of(plane * rows_plane + index * count, count)
            copies.append(
                pltpu.make_async_copy(
                    piece.at[pl.ds(plane * count, count)], template_out.at[pl.ds(start, count)], sems.at[2 * at + plane]
                )
            )
    for copy in copies:
        copy.start()
    rows = 32
    for plane in range(2):
        def step(block, carry):
            at = pl.ds(pl.multiple_of(block * rows, rows), rows)
            image = image_ref[pl.ds(pl.multiple_of(plane * rows_plane + block * rows, rows), rows), :]
            if plane == 0:
                centre, back, ahead = plane_0[at, :], jnp.where(device > 0, before[at, :], 0.0), plane_1[at, :]
            else:
                centre, back, ahead = plane_1[at, :], plane_0[at, :], jnp.where(device < last, after[at, :], 0.0)
            held[plane, at, :] = (image - centre) * (0.5 * (ahead - back))
            return carry

        lax.fori_loop(0, rows_plane // rows, step, 0)
        copy = pltpu.make_async_copy(held.at[plane], out.at[0, plane], sems.at[4 * RING + plane])
        copy.start()
        copies.append(copy)
    for copy in copies:
        copy.wait()


def on_device(template, images, fractions, requests, corners):
    _, plane_count, row_count, cell_count = images.shape
    line_count = plane_count * row_count
    band_count, capacity = requests.shape[2:]
    slab = lax.axis_index("slab")
    subject = lax.axis_index("subj")
    last = lax.axis_size("slab") - 1
    here = slab % RING
    core = subject % 2
    chip = subject // 2
    fixed = [last, lax.axis_size("subj"), line_count, cell_count // LANES]
    place = jnp.stack([here, core, slab, fixed[0], chip, fixed[1], fixed[2], fixed[3]]).astype(I32)
    lists = requests.reshape(band_count, capacity)
    lines = template.reshape(line_count, cell_count)
    parts = cell_count // LANES
    packed = f32s(capacity * parts, LANES)

    message = jax.ShapeDtypeStruct((2, capacity), I32)
    self_lists, *messages = call(
        request_kernel, (jax.ShapeDtypeStruct((3, capacity), I32),) + (message,) * 3, [SMEM, VMEM], (VMEM,) * 4,
    )(place, lists)
    plane = call(
        spread_plane_kernel, f32s(row_count * parts, LANES), [SMEM, VMEM], VMEM,
    )(place, lines)
    spread = call(spread_kernel, f32s(line_count * parts, LANES), [VMEM], VMEM)(lines)
    from_low = along_z(plane, 1)
    from_high = along_z(plane, -1)
    asked = [self_lists] + lax.optimization_barrier(ring_of(along_x, messages, -1))

    own_1, own_3 = call(
        near_lines_kernel, (packed,) * 2, [SMEM] * 2 + [VMEM], (VMEM,) * 2,
    )(asked[1], asked[3], spread)
    got_1, got_3 = along_x(own_1, 1), along_x(own_3, 3)
    own_2 = call(far_lines_kernel, packed, [SMEM, VMEM], VMEM)(asked[2], spread)
    from_low, from_high, own_2, _ = lax.optimization_barrier((from_low, from_high, own_2, (got_1, got_3)))
    got_own = [got_1, along_x(own_2, 2), got_3]
    from_low_b, from_high_b = other_core(from_low), other_core(from_high)
    slabs = (from_low, from_low_b, from_high, from_high_b)
    held_slabs = [pltpu.VMEM((2 * line_count * parts, LANES), F32)]
    cross = call(
        cross_lines_kernel, (packed,) * 3, [SMEM] * 3 + [VMEM] * 4, (VMEM,) * 3, held_slabs,
    )(*asked[1:], *slabs)
    got_cross = ring_of(along_x, cross, 1)
    self_low, self_high, self_own = call(
        self_lines_kernel, (packed,) * 3, [SMEM] + [VMEM] * 5, (VMEM,) * 3, held_slabs,
    )(self_lists, spread, *slabs)

    slot_ids = corners.reshape(4, line_count)
    offset = slot_ids // capacity - REACH
    source = here + offset
    outside = (source < 0) | (source >= RING)
    behind = (here - source) % RING
    held_at = jnp.where(
        behind == 0,
        jnp.where(offset == 0, 8, jnp.where(offset < 0, 3, 4)),
        behind + jnp.where(outside, -1, 4),
    )
    slot_ids = held_at * capacity + slot_ids % capacity
    flat_ids = slot_ids.reshape(1, 4 * line_count)
    blocks = got_cross + [self_low, self_high] + got_own + [self_own]
    here_part, ahead_part = call(
        weight_kernel, (f32s(4, line_count, cell_count),) * 2, [VMEM], (VMEM,) * 2,
    )(fractions.reshape(3, line_count, cell_count))
    half = f32s(row_count, cell_count)
    push_part = jax.ShapeDtypeStruct((4 * line_count, cell_count), BF16)
    warped_0, warped_1, push_high, push_low = call(
        warp_kernel,
        (half,) * 2 + (push_part,) * 2,
        [SMEM] + [VMEM] * 12,
        (VMEM,) * 4,
        [
            pltpu.VMEM((band_count * capacity * parts, LANES), F32),
            pltpu.VMEM((4 * WARP_ROWS * parts, LANES), F32),
            pltpu.VMEM((4 * WARP_ROWS * parts, LANES), F32),
        ],
    )(slot_ids * parts, here_part, ahead_part, images.reshape(line_count, cell_count), *blocks)

    block = f32s(capacity, cell_count)
    pool_cross = call(
        functools.partial(slot_sum_kernel, 0), (block,) * 3, [VMEM] * 3, (VMEM,) * 3,
    )(flat_ids, push_high, push_low)
    pool_low, pool_high, *pool_own = call(
        functools.partial(slot_sum_kernel, 3), (block,) * 6, [VMEM] * 3, (VMEM,) * 6,
    )(flat_ids, push_high, push_low)
    back_cross = ring_of(along_x, pool_cross, -1)
    image_lines = images.reshape(line_count, cell_count)
    force = f32s(3, plane_count, row_count, cell_count)
    part_force = call(
        plane_force_kernel, force, [VMEM] * 3, ANY,
        [pltpu.VMEM((2, plane_count, row_count, cell_count), F32), pltpu.SemaphoreType.DMA],
    )(warped_0, warped_1, image_lines)
    back_cross, pool_own = lax.optimization_barrier((back_cross, pool_own))
    back_own = ring_of(along_x, pool_own, -1)

    per_piece = row_count // (2 * RING)
    wide = per_piece + 2 * HALO
    at = jnp.arange(2 * RING * 2 * wide, dtype=I32)
    piece = at // (2 * wide)
    part = jnp.where(piece < RING, core, 1 - core)
    index = part * RING + (chip + piece) % RING
    row = index * per_piece - HALO + at % wide
    target = jnp.where((row >= 0) & (row < row_count), at // wide % 2 * row_count + row, -(2**20))
    target = target.reshape(-1, 1)
    core_part = f32s(RING * 2 * wide, cell_count)
    core_rows = core_part.shape[0]
    all_rows = 2 * core_rows
    hot_own, hot_low, hot_high = call(
        line_hot_kernel,
        (jax.ShapeDtypeStruct((all_rows, 8 * capacity), BF16),) + (jax.ShapeDtypeStruct((all_rows, 10 * capacity), BF16),) * 2,
        [SMEM] + [VMEM] * 5, (VMEM,) * 3,
    )(place, *asked, target)
    send, stacked = call(
        cross_send_kernel,
        (f32s(2 * core_rows, cell_count), jax.ShapeDtypeStruct((10 * capacity, cell_count), BF16)),
        [VMEM] * 7, (VMEM,) * 2,
    )(hot_low, hot_high, pool_low, pool_high, *back_cross)
    keep_low, keep_high = call(
        cross_keep_kernel, (core_part,) * 2, [VMEM] * 3, (VMEM,) * 2,
    )(hot_low, hot_high, stacked)
    received = other_core(send)
    sum_low = keep_low + received[:core_rows]
    sum_high = keep_high + received[core_rows:]
    in_from_high = along_z(sum_low, -1)
    in_from_low = along_z(sum_high, 1)
    back_own, sum_low, sum_high, part_force = lax.optimization_barrier((back_own, sum_low, sum_high, part_force))
    size = 2 * wide
    keep_own, *send_own = call(
        own_back_kernel, (core_part, f32s(core_rows - size, cell_count), f32s(size, cell_count)),
        [VMEM] * 5, (VMEM,) * 3,
    )(hot_own, pool_own[3], *back_own)
    got_parts = [other_core(part) for part in send_own]
    pieces = [
        keep_own[at * size:(at + 1) * size]
        + (got_parts[0][at * size:(at + 1) * size] if at < RING - 1 else got_parts[1])
        + in_from_high[at * size:(at + 1) * size]
        + in_from_low[at * size:(at + 1) * size]
        for at in range(RING)
    ]
    got_pieces = ring_of(along_y, pieces[1:], 1)
    piece_sum = pieces[0] + got_pieces[0] + got_pieces[1] + got_pieces[2]
    edge_0, edge_1, _ = lax.optimization_barrier((warped_0, warped_1, piece_sum))
    edge_before, edge_after = along_slab(edge_1, 1), along_slab(edge_0, -1)
    before, after = along_slab(piece_sum, 1), along_slab(piece_sum, -1)
    new_piece = call(
        smooth_kernel, f32s(2 * per_piece, cell_count), [SMEM] + [VMEM] * 4, VMEM,
        [pltpu.VMEM((3 * size, cell_count), F32)],
    )(place, before, piece_sum, after, lines)

    mine = [new_piece] + ring_of(along_y, [new_piece] * 3, 1)
    theirs = [other_core(value) for value in mine]
    new_template, image_force = call(
        finish_kernel, (f32s(line_count, cell_count), force), [SMEM] + [VMEM] * 5 + [ANY] * 9, (ANY, ANY),
        [pltpu.VMEM((plane_count, row_count, cell_count), F32), pltpu.SemaphoreType.DMA((4 * RING + 2,))],
        {14: 1},
    )(place, edge_before, warped_0, warped_1, edge_after, image_lines, *mine, *theirs, part_force)
    return new_template.reshape(template.shape), image_force[None]


def solution(mesh):
    return jax.shard_map(
        on_device,
        mesh=mesh,
        in_specs=(
            P("slab", None, None),
            P("subj", "slab", None, None),
            P("subj", None, "slab", None, None),
            P("subj", "slab", None, None),
            P("subj", None, "slab", None),
        ),
        out_specs=(P("slab", None, None), P("subj", None, "slab", None, None)),
        check_vma=False,
    )
```
